256 devices in a mesh: tensor: 32 (over x, z), context: 2 (over core), dp: 4 (over y).
Axes of the slice: x: 4, y: 4, z: 8, core: 2. Of those that a mesh axis runs over, the one named last changes fastest.
Arguments:
- hidden_prev: bfloat16 [1024, 7168], P(('context', 'dp'), 'tensor'), may hold values from -300 to 300
- next_ids: int32 [1024], P(('context', 'dp')), may hold values from 0 to 65535
- targets: int32 [1024], P(('context', 'dp')), may hold values from 0 to 65535
- loss_mask: int32 [1024], P(('context', 'dp')), may hold values from 0 to 1, as said below
- gain_hidden: bfloat16 [7168], P('tensor'), may hold values from 0.099609375 to 1.8984375
- gain_embed: bfloat16 [7168], P('tensor'), may hold values from 0.099609375 to 1.8984375
- gain_final: bfloat16 [7168], P(('context', 'dp')), may hold values from 0.099609375 to 1.8984375
- embed_table: bfloat16 [65536, 7168], P(('context', 'dp'), 'tensor'), may hold values from -200 to 200
- proj_hidden: bfloat16 [7168, 7168], P('tensor', ('context', 'dp')), may hold values from -0.046875 to 0.046875
- proj_embed: bfloat16 [7168, 7168], P('tensor', ('context', 'dp')), may hold values from -0.046875 to 0.046875
- head_weight: bfloat16 [7168, 65536], P(('context', 'dp'), 'tensor'), may hold values from -8 to 8
Outputs:
- loss_value: float32 [], replicated
- hidden_grad: bfloat16 [1024, 7168], P(('context', 'dp'), 'tensor')
- proj_hidden_grad: bfloat16 [7168, 7168], P('tensor', ('context', 'dp'))
- proj_embed_grad: bfloat16 [7168, 7168], P('tensor', ('context', 'dp'))
- head_grad: bfloat16 [7168, 65536], P(('context', 'dp'), 'tensor')
The draws below stay inside these ranges and needn't reach their ends.
Inputs may be any that keep to these rules, and one draw needn't show every extreme that they name: `loss_mask`: the last token always counts.
All inputs are finite; a program needn't handle non-finite values.
Results may differ from the reference program's by a relative error of at most 0.011.
The reference program's roundings to bfloat16 on the way (of `normed_hidden`, `embedded`, `normed_embed`, `final_normed`, `logit_grad` and `mixed_grad`) count: a program that leaves them out, or rounds other values in their place, can miss the bound.
Values may be sent and summed in bfloat16 or wider, within the bound.
A program may use at most 128 MiB of HBM per device.

```python
import math
import jax
import jax.numpy as jnp
import numpy as np
from jax import lax

D = 7168
TOKENS = 1024
VOCAB = 65536


def draw_hidden_prev(key, part):
    key = jax.random.fold_in(key, 11)
    first_key, second_key = jax.random.split(key)
    feature = jnp.arange(D, dtype=jnp.float32)[None, :] / D
    base = jnp.clip(jax.random.normal(first_key, (TOKENS, D), jnp.float32), -6.0, 6.0)
    rising = jnp.exp(2.3 * feature)
    row_scale = jnp.exp(jax.random.uniform(second_key, (TOKENS, 1), jnp.float32, 0.0, 2.3))
    return (base * rising * row_scale / 3.0).astype(jnp.bfloat16)


def draw_embed_table(key, part):
    key = jax.random.fold_in(key, 12)
    first_key, second_key = jax.random.split(key)
    feature = jnp.arange(D, dtype=jnp.float32)[None, :] / D
    base = jnp.clip(jax.random.normal(first_key, (VOCAB, D), jnp.float32), -6.0, 6.0)
    rising = jnp.exp(2.3 * feature)
    row_scale = jnp.exp(jax.random.uniform(second_key, (VOCAB, 1), jnp.float32, 0.0, 2.3))
    return (0.3 * base * rising * row_scale).astype(jnp.bfloat16)


def draw_head_weight(key, part):
    key = jax.random.fold_in(key, 13)
    first_key = jax.random.fold_in(key, 0)
    column_scale = 3.0 / D ** 0.5
    values = jnp.clip(jax.random.normal(first_key, (D, VOCAB), jnp.float32), -6.0, 6.0) * column_scale
    return values.astype(jnp.bfloat16)


def draw_loss_mask(key, part):
    key = jax.random.fold_in(key, 17)
    position = jnp.arange(TOKENS, dtype=jnp.int32)
    ticket = jax.random.randint(key, (TOKENS,), 0, 1000)
    threshold = 250 + 650 * position // TOKENS
    counted = (ticket < threshold).astype(jnp.int32)
    return jnp.where(position == TOKENS - 1, 1, counted).astype(jnp.int32)


def set_ends(array, own_key, low, high):
    extent = array.shape
    spot = [jax.random.randint(jax.random.fold_in(own_key, axis), (), 0, extent[axis]) for axis in range(len(extent))]
    array = array.at[tuple(spot)].set(low)
    longest = extent.index(max(extent))
    spot[longest] = (spot[longest] + 1) % extent[longest]
    return array.at[tuple(spot)].set(high)


def block_levels(rng, extent, pieces, low, high):
    factor_of = 1.0
    for dim, shards_of in pieces:
        heights = jax.random.uniform(jax.random.fold_in(jax.random.fold_in(rng, 6), dim), (shards_of,), jnp.float32, low / len(pieces), high / len(pieces))
        factor_of = factor_of * jnp.repeat(jnp.exp(heights), extent[dim] // shards_of).reshape((-1,) + (1,) * (len(extent) - 1 - dim))
    return factor_of


def rank_bounds(number_of, skew):
    loads = [(1 << 20) // math.isqrt(standing ** skew) + 1 for standing in range(1, number_of + 1)]
    deviation = 1 + sum(loads) // (1 << 30)
    return np.cumsum(np.array([max(1, weight // deviation) for weight in loads]))


def ranked_ids(key, extent, number_of, lean):
    listing = rank_bounds(number_of, lean)
    pick = jax.random.randint(jax.random.fold_in(key, 1), extent, 0, int(listing[number_of - 1]))
    rank = jnp.searchsorted(jnp.asarray(listing, jnp.int32), pick, side="right")
    return jax.random.permutation(jax.random.fold_in(key, 2), number_of)[rank].astype(jnp.int32)


def bell_draw(stream_key, shape, scale, most, shards=(), held_as=jnp.bfloat16):
    level = block_levels(stream_key, shape, shards, -0.22, 0.18) if shards else 1.0
    entries = jax.random.normal(stream_key, shape, jnp.float32) * scale * level
    return jnp.minimum(jnp.maximum(entries, -most), most).astype(held_as)


def setup_inputs(seed: int = 0) -> dict:
    arg_keys = jax.random.split(jax.random.key(seed), 12)
    return {
        "hidden_prev": draw_hidden_prev(jax.random.fold_in(arg_keys[11], 71), 0),
        "next_ids": set_ends(ranked_ids(arg_keys[1], (TOKENS,), VOCAB, 2), jax.random.fold_in(arg_keys[1], 3), 0, VOCAB - 1).astype(jnp.int32),
        "targets": set_ends(ranked_ids(arg_keys[2], (TOKENS,), VOCAB, 2), jax.random.fold_in(arg_keys[2], 3), 0, VOCAB - 1).astype(jnp.int32),
        "loss_mask": draw_loss_mask(jax.random.fold_in(arg_keys[11], 71), 0),
        "gain_hidden": jnp.clip(1.0 + 0.18 * jax.random.normal(arg_keys[4], (D,), jnp.float32), 0.099609375, 1.8984375).astype(jnp.bfloat16),
        "gain_embed": jnp.clip(1.0 + 0.18 * jax.random.normal(arg_keys[5], (D,), jnp.float32), 0.099609375, 1.8984375).astype(jnp.bfloat16),
        "gain_final": jnp.clip(1.0 + 0.18 * jax.random.normal(arg_keys[6], (D,), jnp.float32), 0.099609375, 1.8984375).astype(jnp.bfloat16),
        "embed_table": draw_embed_table(jax.random.fold_in(arg_keys[11], 71), 0),
        "proj_hidden": bell_draw(arg_keys[8], (D, D), (2 * D) ** -0.5, 0.046875, ((0, 32), (1, 8))),
        "proj_embed": bell_draw(arg_keys[9], (D, D), (2 * D) ** -0.5, 0.046875, ((0, 32), (1, 8))),
        "head_weight": draw_head_weight(jax.random.fold_in(arg_keys[11], 71), 0),
    }


EPS = 1e-06

def reference(hidden_prev, next_ids, targets, loss_mask, gain_hidden, gain_embed, gain_final, embed_table, proj_hidden, proj_embed, head_weight):
    hidden = hidden_prev.astype(jnp.float32)
    hidden_rms = jnp.sqrt(lax.optimization_barrier(jnp.mean(hidden * hidden, axis=1, keepdims=True)) + EPS)
    hidden_unit = hidden / hidden_rms
    normed_hidden = (hidden_unit * gain_hidden.astype(jnp.float32)).astype(jnp.bfloat16)
    embedded = jnp.take(embed_table, next_ids.astype(jnp.int32), axis=0).astype(jnp.float32)
    embed_rms = jnp.sqrt(lax.optimization_barrier(jnp.mean(embedded * embedded, axis=1, keepdims=True)) + EPS)
    normed_embed = (embedded / embed_rms * gain_embed.astype(jnp.float32)).astype(jnp.bfloat16)
    mixed = jnp.dot(normed_hidden, proj_hidden, preferred_element_type=jnp.float32) + jnp.dot(normed_embed, proj_embed, preferred_element_type=jnp.float32)
    mixed_rms = jnp.sqrt(lax.optimization_barrier(jnp.mean(mixed * mixed, axis=1, keepdims=True)) + EPS)
    mixed_unit = mixed / mixed_rms
    final_normed = (mixed_unit * gain_final.astype(jnp.float32)).astype(jnp.bfloat16)
    logits = jnp.dot(final_normed, head_weight, preferred_element_type=jnp.float32)
    row_top = lax.optimization_barrier(jnp.max(logits, axis=1, keepdims=True))
    log_total = row_top[:, 0] + jnp.log(lax.optimization_barrier(jnp.sum(jnp.exp(logits - row_top), axis=1)))
    columns = lax.broadcasted_iota(jnp.int32, (1, logits.shape[1]), 1)
    target_hits = columns == targets.astype(jnp.int32)[:, None]
    picked = lax.optimization_barrier(jnp.sum(jnp.where(target_hits, logits, jnp.float32(0.0)), axis=1))
    mask_weights = loss_mask.astype(jnp.float32)
    mask_total = jnp.sum(mask_weights)
    loss_value = jnp.sum(mask_weights * (log_total - picked)) / mask_total
    probs = jnp.exp(logits - log_total[:, None])
    logit_grad = ((mask_weights / mask_total)[:, None] * (probs - target_hits.astype(jnp.float32))).astype(jnp.bfloat16)
    head_grad = jnp.dot(final_normed.T, logit_grad, preferred_element_type=jnp.float32).astype(jnp.bfloat16)
    final_grad = jnp.dot(logit_grad, head_weight.T, preferred_element_type=jnp.float32)
    scaled = final_grad * gain_final.astype(jnp.float32)
    inner = lax.optimization_barrier(jnp.mean(scaled * mixed_unit, axis=1, keepdims=True))
    mixed_grad = ((scaled - mixed_unit * inner) / mixed_rms).astype(jnp.bfloat16)
    proj_hidden_grad = jnp.dot(normed_hidden.T, mixed_grad, preferred_element_type=jnp.float32).astype(jnp.bfloat16)
    proj_embed_grad = jnp.dot(normed_embed.T, mixed_grad, preferred_element_type=jnp.float32).astype(jnp.bfloat16)
    normed_hidden_grad = jnp.dot(mixed_grad, proj_hidden.T, preferred_element_type=jnp.float32)
    scaled_hidden = normed_hidden_grad * gain_hidden.astype(jnp.float32)
    inner_hidden = lax.optimization_barrier(jnp.mean(scaled_hidden * hidden_unit, axis=1, keepdims=True))
    hidden_grad = ((scaled_hidden - hidden_unit * inner_hidden) / hidden_rms).astype(jnp.bfloat16)
    return (loss_value, hidden_grad, proj_hidden_grad, proj_embed_grad, head_grad)
```

```python
import functools
import jax
import jax.numpy as jnp
from jax import lax
from jax.experimental import pallas as pl
from jax.experimental.pallas import tpu as pltpu
from jax.sharding import PartitionSpec as P

D = 7168
EPS = 1e-06
MESH = pl.DeviceIdType.MESH
F32 = jnp.float32
BF16 = jnp.bfloat16
NX, NZ, NC, NY = 4, 8, 2, 4
NT, NG = NX * NZ, NC * NY
ROWS = 32
OWN = 128
WIDE = 896
CA = 640
CB = WIDE - CA
FEAT = 224
VOC = 2048
TABLE = 8192
X_ORDER = (2, 1, 3)
Z_ORDER = (4, 3, 5, 2, 6, 1, 7)
VMEM_LIMIT = 60 * 1024 * 1024


def place():
    t = lax.axis_index("tensor")
    return t // NZ, t % NZ, lax.axis_index("context"), lax.axis_index("dp")


def rcopy(src, dst, ss, rs, dev):
    return pltpu.make_async_remote_copy(
        src_ref=src, dst_ref=dst, send_sem=ss, recv_sem=rs, device_id=dev, device_id_type=MESH
    )


def greet_all():
    x, z, c, y = place()
    t = x * NZ + z
    bar = pltpu.get_barrier_semaphore()

    def hello(k, carry):
        pl.semaphore_signal(
            bar, inc=1, device_id={"tensor": (t + k) % NT}, device_id_type=MESH
        )
        return carry

    lax.fori_loop(1, NT, hello, 0)
    for dc in range(NC):
        for dy in range(NY):
            if dc or dy:
                pl.semaphore_signal(
                    bar,
                    inc=1,
                    device_id={"context": (c + dc) % NC, "dp": (y + dy) % NY},
                    device_id_type=MESH,
                )
    pl.semaphore_wait(bar, NT - 1 + NG - 1)


def to_row(col):
    return jnp.broadcast_to(col, (OWN, OWN)).T[:1, :]


def to_col(row):
    return jnp.broadcast_to(row, (OWN, OWN)).T[:, :1]


def share_tensor(tile, recv, ss, rs):
    x, z, _, _ = place()
    t = x * NZ + z
    recv[t] = tile

    def send(k, carry):
        rcopy(recv.at[t], recv.at[t], ss, rs, {"tensor": (t + k) % NT}).start()
        return carry

    lax.fori_loop(1, NT, send, 0)
    every = rcopy(
        recv.at[pl.ds(0, NT - 1)], recv.at[pl.ds(0, NT - 1)], ss, rs, {"tensor": (t + 1) % NT}
    )
    every.wait_recv()
    every.wait_send()


def g_peers():
    _, _, c, y = place()
    for dy in (2, 1, 3, 0):
        for dc in (1, 0):
            if dc or dy:
                cb, yb = (c + dc) % NC, (y + dy) % NY
                yield cb * NY + yb, {"context": cb, "dp": yb}


def share_g(recv, ss, rs):
    _, _, c, y = place()
    g = c * NY + y
    copies = []
    for i, (_, dev) in enumerate(g_peers()):
        copy = rcopy(recv.at[g], recv.at[g], ss.at[i], rs.at[i], dev)
        copy.start()
        copies.append(copy)
    return copies


def scatter_g(src, recv, ss, rs):
    _, _, c, y = place()
    g = c * NY + y
    copies = []
    for i, (gb, dev) in enumerate(g_peers()):
        copy = rcopy(src.at[gb], recv.at[g], ss.at[i], rs.at[i], dev)
        copy.start()
        copies.append(copy)
    return copies


def finish(copies):
    for copy in copies:
        copy.wait()


def gather_g(buf, ssy, rsy, ssc, rsc):
    _, _, c, y = place()
    sibling = {"context": 1 - c}
    own = c * NY + y
    copies, ahead = {}, []
    for dy in (2, 1, 3):
        copies[dy] = rcopy(
            buf.at[own], buf.at[own], ssy.at[dy - 1], rsy.at[dy - 1], {"dp": (y + dy) % NY}
        )
        copies[dy].start()
    cross = rcopy(buf.at[own], buf.at[own], ssc.at[0], rsc.at[0], sibling)
    cross.start()
    ahead.append(cross)
    for dy in (1, 3, 2):
        copies[dy].wait_recv()
        block = c * NY + (y + NY - dy) % NY
        cross = rcopy(buf.at[block], buf.at[block], ssc.at[dy], rsc.at[dy], sibling)
        cross.start()
        ahead.append(cross)
    for copy in ahead:
        copy.wait()
    for dy in (2, 1, 3):
        copies[dy].wait_send()


def reduce_tensor(part, bufs, compute_block, beside=None):
    ra, rb, sa, sb, ra2, rb2, s1, r1, s2, r2 = bufs
    x, z, _, _ = place()
    first, second = {}, {}
    for dx in X_ORDER + (0,):
        xb = (x + dx) % NX
        compute_block(xb)
        if dx:
            first["x", dx] = rcopy(
                part.at[xb, :, :, pl.ds(0, CA)],
                ra.at[x],
                s1.at[dx],
                r1.at[dx],
                {"tensor": xb * NZ + z},
            )
            first["x", dx].start()
    for dz in Z_ORDER:
        zb = (z + dz) % NZ
        first["z", dz] = rcopy(
            part.at[:, zb, :, pl.ds(CA, CB)],
            rb.at[z],
            s1.at[NX + dz],
            r1.at[NX + dz],
            {"tensor": x * NZ + zb},
        )
        first["z", dz].start()
    if beside is not None:
        beside()
    for dx in X_ORDER:
        first["x", dx].wait_recv()
    for dz in Z_ORDER + (0,):
        zb = (z + dz) % NZ
        total = part[x, zb, :, :CA]
        for dx in X_ORDER:
            total = total + ra[(x + NX - dx) % NX, zb]
        sa[zb] = total
        if dz:
            second["z", dz] = rcopy(
                sa.at[zb], ra2.at[z], s2.at[NX + dz], r2.at[NX + dz], {"tensor": x * NZ + zb}
            )
            second["z", dz].start()
    for dz in Z_ORDER:
        first["z", dz].wait_recv()
    for dx in X_ORDER + (0,):
        xb = (x + dx) % NX
        total = part[xb, z, :, CA:]
        for dz in Z_ORDER:
            total = total + rb[(z + NZ - dz) % NZ, xb]
        sb[xb] = total
        if dx:
            second["x", dx] = rcopy(
                sb.at[xb], rb2.at[x], s2.at[dx], r2.at[dx], {"tensor": xb * NZ + z}
            )
            second["x", dx].start()
    for copy in second.values():
        copy.wait_recv()
    left, right = sa[z], sb[x]
    for dz in Z_ORDER:
        left = left + ra2[(z + NZ - dz) % NZ]
    for dx in X_ORDER:
        right = right + rb2[(x + NX - dx) % NX]
    for copy in list(first.values()) + list(second.values()):
        copy.wait_send()
    return left, right


def reduce_scratch():
    return [
        pltpu.VMEM((NX, NZ, ROWS, CA), F32),
        pltpu.VMEM((NZ, NX, ROWS, CB), F32),
        pltpu.VMEM((NZ, ROWS, CA), F32),
        pltpu.VMEM((NX, ROWS, CB), F32),
        pltpu.VMEM((NZ, ROWS, CA), F32),
        pltpu.VMEM((NX, ROWS, CB), F32),
    ] + [pltpu.SemaphoreType.DMA((NX + NZ,))] * 4


def gather_tensor(buf, s1, r1, s2, r2):
    x, z, _, _ = place()
    left, right = pl.ds(0, CA), pl.ds(CA, CB)
    copies = {}

    def go(ref, ss, rs, name, slot, peer):
        copies[name] = rcopy(ref, ref, ss.at[slot], rs.at[slot], {"tensor": peer})
        copies[name].start()

    for dz in Z_ORDER:
        go(buf.at[x, z, :, left], s1, r1, (1, "z", dz), NX + dz, x * NZ + (z + dz) % NZ)
    for dx in X_ORDER:
        go(buf.at[x, z, :, right], s1, r1, (1, "x", dx), dx, (x + dx) % NX * NZ + z)
    for dx in X_ORDER:
        copies[1, "x", dx].wait_recv()
    for dz in Z_ORDER:
        go(buf.at[:, z, :, right], s2, r2, (2, "z", dz), NX + dz, x * NZ + (z + dz) % NZ)
    for dz in Z_ORDER:
        copies[1, "z", dz].wait_recv()
    for dx in X_ORDER:
        go(buf.at[x, :, :, left], s2, r2, (2, "x", dx), dx, (x + dx) % NX * NZ + z)
    for name, copy in copies.items():
        if name[0] == 2:
            copy.wait_recv()
    for copy in copies.values():
        copy.wait_send()


def rms(squares):
    return jnp.sqrt(squares / D + EPS)


def front_kernel(
    hidden_ref,
    ids_ref,
    gain_h_ref,
    gain_e_ref,
    gain_f_ref,
    table_ref,
    proj_h_ref,
    proj_e_ref,
    nh_ref,
    ne_ref,
    fn_ref,
    unit_ref,
    mrms_ref,
    hrms_ref,
    ids_all,
    ids_col,
    look,
    look_recv,
    stats,
    part,
    squares,
    ids_s,
    ids_r,
    emb_s,
    emb_r,
    st_s,
    st_r,
    gy_s,
    gy_r,
    gc_s,
    gc_r,
    sq_s,
    sq_r,
    ag_s1,
    ag_r1,
    ag_s2,
    ag_r2,
    *reduce_bufs,
):
    x, z, c, y = place()
    g = c * NY + y
    greet_all()
    ids_all[g] = ids_ref[...]
    sent_ids = share_g(ids_all, ids_s, ids_r)
    hidden = hidden_ref[...].astype(F32)
    hidden_squares = jnp.sum(hidden * hidden, axis=1, keepdims=True)
    finish(sent_ids)
    for b in range(NG):
        ids_col[pl.ds(b * OWN, OWN), :] = to_col(ids_all[b]) - g * TABLE

    step = 1024
    slab = 256

    def lookup(b, carry):
        column = ids_col[pl.ds(pl.multiple_of(b * slab, slab), slab), :]

        def chunk(k, total):
            hits = column == lax.broadcasted_iota(jnp.int32, (slab, step), 1) + k * step
            ones = jnp.where(hits, F32(1.0), F32(0.0)).astype(BF16)
            rows = table_ref[pl.ds(pl.multiple_of(k * step, step), step), :]
            return total + jnp.dot(ones, rows, preferred_element_type=F32)

        total = lax.fori_loop(0, TABLE // step, chunk, jnp.zeros((slab, FEAT), F32))
        look[pl.ds(b * 2, 2)] = total.astype(BF16).reshape(2, OWN, FEAT)
        return carry

    lax.fori_loop(0, NG * OWN // slab, lookup, 0)
    sent = scatter_g(look, look_recv, emb_s, emb_r)
    look_recv[g] = look[g]
    finish(sent)
    embedded = look_recv[0].astype(F32)
    for b in range(1, NG):
        embedded = embedded + look_recv[b].astype(F32)
    embed_squares = jnp.sum(embedded * embedded, axis=1, keepdims=True)
    tile = jnp.concatenate(
        [to_row(hidden_squares), to_row(embed_squares), jnp.zeros((6, OWN), F32)], axis=0
    )
    share_tensor(tile, stats, st_s, st_r)
    sums = jnp.sum(stats[...], axis=0)
    hidden_rms = rms(to_col(sums[:1, :]))
    embed_rms = rms(to_col(sums[1:2, :]))
    hrms_ref[...] = hidden_rms
    nh_ref[g] = (hidden / hidden_rms * gain_h_ref[...].astype(F32)).astype(BF16)
    ne_ref[g] = (embedded / embed_rms * gain_e_ref[...].astype(F32)).astype(BF16)
    gather_g(nh_ref, gy_s.at[0], gy_r.at[0], gc_s.at[0], gc_r.at[0])
    gather_g(ne_ref, gy_s.at[1], gy_r.at[1], gc_s.at[1], gc_r.at[1])

    def project(xb):
        nh = nh_ref[pl.ds(xb * 2, 2)].reshape(2 * OWN, FEAT)
        ne = ne_ref[pl.ds(xb * 2, 2)].reshape(2 * OWN, FEAT)
        terms = jnp.dot(nh, proj_h_ref[...], preferred_element_type=F32) + jnp.dot(
            ne, proj_e_ref[...], preferred_element_type=F32
        )
        part[xb] = terms.reshape(NZ, ROWS, WIDE)

    left, right = reduce_tensor(part, reduce_bufs, project)
    own_squares = jnp.sum(left * left, axis=1, keepdims=True) + jnp.sum(
        right * right, axis=1, keepdims=True
    )
    squares[g] = jnp.broadcast_to(own_squares, (ROWS, OWN))
    finish(share_g(squares, sq_s, sq_r))
    mixed_rms = rms(jnp.sum(squares[...], axis=0)[:, :1])
    mrms_ref[...] = mixed_rms
    left, right = left / mixed_rms, right / mixed_rms
    unit_ref[:, :CA] = left
    unit_ref[:, CA:] = right
    gain = gain_f_ref[...].astype(F32)
    fn_ref[x, z, :, :CA] = (left * gain[:, :CA]).astype(BF16)
    fn_ref[x, z, :, CA:] = (right * gain[:, CA:]).astype(BF16)
    gather_tensor(fn_ref, ag_s1, ag_r1, ag_s2, ag_r2)


def vmem(n):
    return [pl.BlockSpec(memory_space=pltpu.VMEM)] * n


def dma(*shape):
    return pltpu.SemaphoreType.DMA(shape)


def params(cid):
    return pltpu.CompilerParams(
        collective_id=cid, has_side_effects=True, vmem_limit_bytes=VMEM_LIMIT
    )


def front(hidden, ids, gain_h, gain_e, gain_f, table, proj_h, proj_e):
    return pl.pallas_call(
        front_kernel,
        out_shape=(
            jax.ShapeDtypeStruct((NG, OWN, FEAT), BF16),
            jax.ShapeDtypeStruct((NG, OWN, FEAT), BF16),
            jax.ShapeDtypeStruct((NX, NZ, ROWS, WIDE), BF16),
            jax.ShapeDtypeStruct((ROWS, WIDE), F32),
            jax.ShapeDtypeStruct((ROWS, 1), F32),
            jax.ShapeDtypeStruct((OWN, 1), F32),
        ),
        in_specs=vmem(8),
        out_specs=tuple(vmem(6)),
        scratch_shapes=[
            pltpu.VMEM((NG, 1, OWN), jnp.int32),
            pltpu.VMEM((NG * OWN, 1), jnp.int32),
            pltpu.VMEM((NG, OWN, FEAT), BF16),
            pltpu.VMEM((NG, OWN, FEAT), BF16),
            pltpu.VMEM((NT, 8, OWN), F32),
            pltpu.VMEM((NX, NZ, ROWS, WIDE), F32),
            pltpu.VMEM((NG, ROWS, OWN), F32),
            dma(NG - 1),
            dma(NG - 1),
            dma(NG - 1),
            dma(NG - 1),
            pltpu.SemaphoreType.DMA,
            pltpu.SemaphoreType.DMA,
            dma(2, 3),
            dma(2, 3),
            dma(2, 4),
            dma(2, 4),
            dma(NG - 1),
            dma(NG - 1),
        ]
        + [dma(NX + NZ)] * 4
        + reduce_scratch(),
        compiler_params=params(0),
        name="front",
    )(hidden, ids, gain_h, gain_e, gain_f, table, proj_h, proj_e)


CHUNKS = 4
CW = VOC // CHUNKS


def middle_kernel(
    fn_ref,
    head_ref,
    targets_ref,
    mask_ref,
    lg_ref,
    loss_ref,
    logits,
    core_recv,
    y_recv,
    stats,
    masks,
    losses,
    mk_s,
    mk_r,
    co_s,
    co_r,
    ry_s,
    ry_r,
    st_s,
    st_r,
    lo_s,
    lo_r,
    gy_s,
    gy_r,
    gc_s,
    gc_r,
):
    x, z, c, y = place()
    g = c * NY + y
    greet_all()
    mask = mask_ref[...].astype(F32)
    masks[g] = jnp.broadcast_to(mask, (8, OWN))
    sent_masks = share_g(masks, mk_s, mk_r)
    half = NY * OWN
    other = 1 - c

    def product(core, n):
        rows = fn_ref[pl.ds(core * 2, 2)].reshape(half, WIDE)
        terms = jnp.dot(
            rows, head_ref[:, n * CW : (n + 1) * CW], preferred_element_type=F32
        )
        logits[core, :, :, n * CW : (n + 1) * CW] = terms.reshape(NY, OWN, CW)

    crossing = []
    for n in range(CHUNKS):
        product(other, n)
        columns = pl.ds(n * CW, CW)
        copy = rcopy(
            logits.at[other, :, :, columns],
            core_recv.at[:, :, columns],
            co_s.at[n],
            co_r.at[n],
            {"context": other},
        )
        copy.start()
        crossing.append(copy)
    along = []
    for n in range(CHUNKS):
        product(c, n)
        columns = pl.ds(n * CW, CW)
        crossing[n].wait_recv()
        logits[c, :, :, columns] = logits[c, :, :, columns] + core_recv[:, :, columns]
        for dy in (2, 1, 3):
            yb = (y + dy) % NY
            copy = rcopy(
                logits.at[c, yb, :, columns],
                y_recv.at[dy - 1, :, columns],
                ry_s.at[n, dy - 1],
                ry_r.at[n, dy - 1],
                {"dp": yb},
            )
            copy.start()
            along.append(copy)
    target = to_col(targets_ref[...])
    finish(sent_masks)
    mask_total = jnp.sum(masks[...][:, :1, :])
    for copy in along:
        copy.wait_recv()
    for copy in along + crossing:
        copy.wait_send()
    own = logits[c, y] + y_recv[0] + y_recv[1] + y_recv[2]
    columns = lax.broadcasted_iota(jnp.int32, (1, VOC), 1) + (x * NZ + z) * VOC
    hits = columns == target
    top = jnp.max(own, axis=1, keepdims=True)
    total = jnp.sum(jnp.exp(own - top), axis=1, keepdims=True)
    picked = jnp.sum(jnp.where(hits, own, F32(0.0)), axis=1, keepdims=True)
    tile = jnp.concatenate(
        [to_row(top), to_row(total), to_row(picked), jnp.zeros((5, OWN), F32)], axis=0
    )
    share_tensor(tile, stats, st_s, st_r)
    every = stats[...]
    tops = every[:, 0, :]
    row_top = jnp.max(tops, axis=0, keepdims=True)
    exp_total = jnp.sum(every[:, 1, :] * jnp.exp(tops - row_top), axis=0, keepdims=True)
    picked = jnp.sum(every[:, 2, :], axis=0, keepdims=True)
    log_total = row_top + jnp.log(exp_total)
    losses[g] = jnp.broadcast_to(
        jnp.sum(mask * (log_total - picked), axis=1, keepdims=True), (8, OWN)
    )
    sent_losses = share_g(losses, lo_s, lo_r)
    probs = jnp.exp(own - to_col(log_total))
    weight = to_col(mask / mask_total)
    lg_ref[g] = (weight * (probs - jnp.where(hits, F32(1.0), F32(0.0)))).astype(BF16)
    gather_g(lg_ref, gy_s, gy_r, gc_s, gc_r)
    finish(sent_losses)
    loss_ref[...] = jnp.sum(losses[...], axis=0)[:1, :1] / mask_total


def middle(fn, head, targets, mask):
    return pl.pallas_call(
        middle_kernel,
        out_shape=(
            jax.ShapeDtypeStruct((NG, OWN, VOC), BF16),
            jax.ShapeDtypeStruct((1, 1), F32),
        ),
        in_specs=vmem(4),
        out_specs=tuple(vmem(2)),
        scratch_shapes=[
            pltpu.VMEM((NC, NY, OWN, VOC), F32),
            pltpu.VMEM((NY, OWN, VOC), F32),
            pltpu.VMEM((NY - 1, OWN, VOC), F32),
            pltpu.VMEM((NT, 8, OWN), F32),
            pltpu.VMEM((NG, 8, OWN), F32),
            pltpu.VMEM((NG, 8, OWN), F32),
            dma(NG - 1),
            dma(NG - 1),
            dma(CHUNKS),
            dma(CHUNKS),
            dma(CHUNKS, 3),
            dma(CHUNKS, 3),
            pltpu.SemaphoreType.DMA,
            pltpu.SemaphoreType.DMA,
            dma(NG - 1),
            dma(NG - 1),
            dma(3),
            dma(3),
            dma(4),
            dma(4),
        ],
        compiler_params=params(1),
        name="middle",
    )(fn, head, targets, mask)


def back_kernel(
    lg_ref,
    fn_ref,
    head_ref,
    unit_ref,
    mrms_ref,
    gain_f_ref,
    nh_ref,
    ne_ref,
    proj_h_ref,
    hidden_ref,
    hrms_ref,
    gain_h_ref,
    hidden_grad_ref,
    ph_grad_ref,
    pe_grad_ref,
    head_grad_ref,
    part,
    flipped,
    inners,
    mg,
    nhg,
    nhg_recv,
    stats,
    in_s,
    in_r,
    ng_s,
    ng_r,
    st_s,
    st_r,
    ag_s1,
    ag_r1,
    ag_s2,
    ag_r2,
    *reduce_bufs,
):
    x, z, c, y = place()
    g = c * NY + y
    greet_all()

    def terms(xb):
        rows = lg_ref[pl.ds(xb * 2, 2)].reshape(2 * OWN, VOC)
        out = lax.dot_general(
            rows, head_ref[...], (((1,), (1,)), ((), ())), preferred_element_type=F32
        )
        part[xb] = out.reshape(NZ, ROWS, WIDE)

    def head_side():
        for xb in range(NX):
            flipped[:, xb * 256 : (xb + 1) * 256] = fn_ref[xb].reshape(256, WIDE).T

        def tile(n, carry):
            columns = pl.ds(pl.multiple_of(n * 256, 256), 256)
            grads = lg_ref[:, :, columns].reshape(NG * OWN, 256)
            head_grad_ref[:, columns] = jnp.dot(
                flipped[...], grads, preferred_element_type=F32
            ).astype(BF16)
            return carry

        lax.fori_loop(0, VOC // 256, tile, 0)

    left, right = reduce_tensor(part, reduce_bufs, terms, head_side)
    gain = gain_f_ref[...].astype(F32)
    left, right = left * gain[:, :CA], right * gain[:, CA:]
    unit = unit_ref[...]
    own_inner = jnp.sum(left * unit[:, :CA], axis=1, keepdims=True) + jnp.sum(
        right * unit[:, CA:], axis=1, keepdims=True
    )
    inners[g] = jnp.broadcast_to(own_inner, (ROWS, OWN))
    finish(share_g(inners, in_s, in_r))
    inner = jnp.sum(inners[...], axis=0)[:, :1] / D
    mixed_rms = mrms_ref[...]
    mg[x, z, :, :CA] = ((left - unit[:, :CA] * inner) / mixed_rms).astype(BF16)
    mg[x, z, :, CA:] = ((right - unit[:, CA:] * inner) / mixed_rms).astype(BF16)
    gather_tensor(mg, ag_s1, ag_r1, ag_s2, ag_r2)
    grads = mg[...].reshape(NG * OWN, WIDE)
    nhg[...] = lax.dot_general(
        grads, proj_h_ref[...], (((1,), (1,)), ((), ())), preferred_element_type=F32
    ).reshape(NG, OWN, FEAT)
    sent = scatter_g(nhg, nhg_recv, ng_s, ng_r)
    nhg_recv[g] = nhg[g]
    over_rows = (((0,), (0,)), ((), ()))
    ph_grad_ref[...] = lax.dot_general(
        nh_ref[...].reshape(NG * OWN, FEAT), grads, over_rows, preferred_element_type=F32
    ).astype(BF16)
    pe_grad_ref[...] = lax.dot_general(
        ne_ref[...].reshape(NG * OWN, FEAT), grads, over_rows, preferred_element_type=F32
    ).astype(BF16)
    finish(sent)
    scaled = jnp.sum(nhg_recv[...], axis=0) * gain_h_ref[...].astype(F32)
    hidden_rms = hrms_ref[...]
    hidden_unit = hidden_ref[...].astype(F32) / hidden_rms
    inner = jnp.sum(scaled * hidden_unit, axis=1, keepdims=True)
    tile = jnp.broadcast_to(to_row(inner), (8, OWN))
    share_tensor(tile, stats, st_s, st_r)
    inner = to_col(jnp.sum(stats[...], axis=0)[:1, :]) / D
    hidden_grad_ref[...] = ((scaled - hidden_unit * inner) / hidden_rms).astype(BF16)


def back(*args):
    return pl.pallas_call(
        back_kernel,
        out_shape=(
            jax.ShapeDtypeStruct((OWN, FEAT), BF16),
            jax.ShapeDtypeStruct((FEAT, WIDE), BF16),
            jax.ShapeDtypeStruct((FEAT, WIDE), BF16),
            jax.ShapeDtypeStruct((WIDE, VOC), BF16),
        ),
        in_specs=vmem(12),
        out_specs=tuple(vmem(4)),
        scratch_shapes=[
            pltpu.VMEM((NX, NZ, ROWS, WIDE), F32),
            pltpu.VMEM((WIDE, NG * OWN), BF16),
            pltpu.VMEM((NG, ROWS, OWN), F32),
            pltpu.VMEM((NX, NZ, ROWS, WIDE), BF16),
            pltpu.VMEM((NG, OWN, FEAT), F32),
            pltpu.VMEM((NG, OWN, FEAT), F32),
            pltpu.VMEM((NT, 8, OWN), F32),
            dma(NG - 1),
            dma(NG - 1),
            dma(NG - 1),
            dma(NG - 1),
            pltpu.SemaphoreType.DMA,
            pltpu.SemaphoreType.DMA,
        ]
        + [dma(NX + NZ)] * 4
        + reduce_scratch(),
        compiler_params=params(2),
        name="back",
    )(*args)


def per_device(
    hidden_prev,
    next_ids,
    targets,
    loss_mask,
    gain_hidden,
    gain_embed,
    gain_final,
    embed_table,
    proj_hidden,
    proj_embed,
    head_weight,
):
    gain_h, gain_e, gain_f = gain_hidden[None, :], gain_embed[None, :], gain_final[None, :]
    nh, ne, fn, unit, mixed_rms, hidden_rms = front(
        hidden_prev, next_ids[None, :], gain_h, gain_e, gain_f, embed_table, proj_hidden, proj_embed
    )
    lg, loss = middle(fn, head_weight, targets[None, :], loss_mask[None, :])
    hidden_grad, ph_grad, pe_grad, head_grad = back(
        lg,
        fn,
        head_weight,
        unit,
        mixed_rms,
        gain_f,
        nh,
        ne,
        proj_hidden,
        hidden_prev,
        hidden_rms,
        gain_h,
    )
    return (loss[0, 0], hidden_grad, ph_grad, pe_grad, head_grad)


def solution(mesh):
    return jax.shard_map(
        per_device,
        mesh=mesh,
        in_specs=(
            P(("context", "dp"), "tensor"),
            P(("context", "dp")),
            P(("context", "dp")),
            P(("context", "dp")),
            P("tensor"),
            P("tensor"),
            P(("context", "dp")),
            P(("context", "dp"), "tensor"),
            P("tensor", ("context", "dp")),
            P("tensor", ("context", "dp")),
            P(("context", "dp"), "tensor"),
        ),
        out_specs=(
            P(),
            P(("context", "dp"), "tensor"),
            P("tensor", ("context", "dp")),
            P("tensor", ("context", "dp")),
            P(("context", "dp"), "tensor"),
        ),
        check_vma=False,
    )
```

```python
from typing import NamedTuple

import jax
import jax.numpy as jnp
from jax import lax
from jax.experimental import pallas as pl
from jax.experimental.pallas import tpu as pltpu
from jax.sharding import PartitionSpec as P

D = 7168
EPS = 1e-06
MESH = pl.DeviceIdType.MESH
F32 = jnp.float32
BF16 = jnp.bfloat16
NX, NZ, NC, NY = 4, 8, 2, 4
NT, NG = NX * NZ, NC * NY
ROWS = 32
OWN = 128
WIDE = 896
FEAT = 224
VOC = 2048
TABLE = 8192
Z_ORDER = (4, 3, 5, 2, 6, 1, 7)
VMEM_LIMIT = 62 * 1024 * 1024
PARTS = 2
R = ROWS // PARTS
TOK = NX * NZ * R
GR = OWN // PARTS
CHUNKS = 2
CW = VOC // CHUNKS


def place():
    t = lax.axis_index("tensor")
    return t // NZ, t % NZ, lax.axis_index("context"), lax.axis_index("dp")


def rcopy(src, dst, ss, rs, dev):
    return pltpu.make_async_remote_copy(
        src_ref=src, dst_ref=dst, send_sem=ss, recv_sem=rs, device_id=dev, device_id_type=MESH
    )


def greet_all():
    x, z, c, y = place()
    t = x * NZ + z
    bar = pltpu.get_barrier_semaphore()

    def hello(k, carry):
        pl.semaphore_signal(
            bar, inc=1, device_id={"tensor": (t + k) % NT}, device_id_type=MESH
        )
        return carry

    lax.fori_loop(1, NT, hello, 0)
    for dc in range(NC):
        for dy in range(NY):
            if dc or dy:
                pl.semaphore_signal(
                    bar,
                    inc=1,
                    device_id={"context": (c + dc) % NC, "dp": (y + dy) % NY},
                    device_id_type=MESH,
                )
    return bar


def to_tile(columns):
    n = columns[0].shape[0]
    lane = lax.broadcasted_iota(jnp.int32, (n, OWN), 1)
    wide = jnp.zeros((n, OWN), F32)
    for i, column in enumerate(columns):
        wide = jnp.where(lane == i, column, wide)
    if n < OWN:
        wide = jnp.concatenate([wide] * (OWN // n), axis=0)
    return wide.T[:8, :]


def to_col(row, n=OWN):
    return jnp.broadcast_to(row, (OWN, OWN)).T[:n, :1]


def share_tensor(tile, recv, ss, rs):
    x, z, _, _ = place()
    t = x * NZ + z
    recv[t] = tile

    def send(k, carry):
        rcopy(recv.at[t], recv.at[t], ss, rs, {"tensor": (t + k) % NT}).start()
        return carry

    lax.fori_loop(1, NT, send, 0)
    return [
        rcopy(
            recv.at[pl.ds(0, NT - 1)], recv.at[pl.ds(0, NT - 1)], ss, rs, {"tensor": (t + 1) % NT}
        )
    ]


def g_peers():
    _, _, c, y = place()
    for dy in (2, 1, 3, 0):
        for dc in (1, 0):
            if dc or dy:
                cb, yb = (c + dc) % NC, (y + dy) % NY
                yield cb * NY + yb, {"context": cb, "dp": yb}


def share_g(recv, ss, rs):
    _, _, c, y = place()
    g = c * NY + y
    copies = []
    for i, (_, dev) in enumerate(g_peers()):
        copy = rcopy(recv.at[g], recv.at[g], ss.at[i], rs.at[i], dev)
        copy.start()
        copies.append(copy)
    return copies


def scatter_g(src, recv, ss, rs):
    _, _, c, y = place()
    g = c * NY + y
    copies = []
    for i, (gb, dev) in enumerate(g_peers()):
        copy = rcopy(src.at[gb], recv.at[g], ss.at[i], rs.at[i], dev)
        copy.start()
        copies.append(copy)
    return copies


def arrive(copies):
    for copy in copies:
        copy.wait_recv()


def finish(copies):
    for copy in copies:
        copy.wait()


def g_block(ref, g):
    return ref.at[g // 2, pl.ds(g % 2 * 4, 4)]


def gather_g(buf, ssy, rsy, ssc, rsc, done):
    _, _, c, y = place()
    own, near = (c * NY + (y + dy) % NY for dy in (0, 1))
    before, far = (c * NY + (y + dy) % NY for dy in (3, 2))
    copies, ahead = [], []

    def go(ref, i, dev):
        copies.append(rcopy(ref, ref, ssy.at[i], rsy.at[i], dev))
        copies[-1].start()

    def cross(block, i):
        ref = g_block(buf, block)
        ahead.append(rcopy(ref, ref, ssc.at[i], rsc.at[i], {"context": 1 - c}))
        ahead[-1].start()

    up, down = {"dp": (y + 1) % NY}, {"dp": (y + 3) % NY}
    go(g_block(buf, own), 0, up)
    go(g_block(buf, own), 1, down)
    cross(own, 0)
    yield
    copies[0].wait_recv()
    go(g_block(buf, before).at[pl.ds(0, 2)], 2, up)
    cross(before, 1)
    copies[1].wait_recv()
    go(g_block(buf, near).at[pl.ds(2, 2)], 3, down)
    cross(near, 2)
    yield
    copies[2].wait_recv()
    copies[3].wait_recv()
    cross(far, 3)
    yield
    arrive(ahead)
    done += ahead + copies


def reduce_tensor(part, bufs, compute_block, done, result):
    first, near, line, last, s1, r1, s2, r2 = bufs
    x, z, _, _ = place()
    low, high = pl.ds(0, NZ // 2), pl.ds(NZ // 2, NZ // 2)
    after, far, before = ((x + dx) % NX for dx in (1, 2, 3))
    up, down = {"tensor": after * NZ + z}, {"tensor": before * NZ + z}
    copies = []

    def go(src, dst, i, dev):
        copies.append(rcopy(src, dst, s1.at[i], r1.at[i], dev))
        copies[-1].start()

    compute_block(far)
    go(part.at[far, low], first.at[0], 0, up)
    go(part.at[far, high], first.at[1], 1, down)
    compute_block(after)
    go(part.at[after, high], near.at[0, high], 2, up)
    compute_block(before)
    go(part.at[before, low], near.at[1, low], 3, down)
    compute_block(x)
    yield
    copies[0].wait_recv()
    part[after, low] = part[after, low] + first[0]
    go(part.at[after, low], near.at[0, low], 4, up)
    copies[1].wait_recv()
    part[before, high] = part[before, high] + first[1]
    go(part.at[before, high], near.at[1, high], 5, down)
    yield
    arrive(copies[2:])
    second = []
    for dz in Z_ORDER + (0,):
        zb = (z + dz) % NZ
        line[zb] = part[x, zb] + near[0, zb] + near[1, zb]
        if dz:
            second.append(
                rcopy(line.at[zb], last.at[z], s2.at[dz], r2.at[dz], {"tensor": x * NZ + zb})
            )
            second[-1].start()
    yield
    arrive(second)
    total = line[z]
    for dz in Z_ORDER:
        total = total + last[(z + NZ - dz) % NZ]
    for copy in copies + second:
        copy.wait_send()
    result.append(total)


def reduce_scratch():
    return [
        pltpu.VMEM((PARTS, NX, NZ, R, WIDE), F32),
        pltpu.VMEM((PARTS, 2, NZ // 2, R, WIDE), F32),
        pltpu.VMEM((PARTS, 2, NZ, R, WIDE), F32),
        pltpu.VMEM((PARTS, NZ, R, WIDE), F32),
        pltpu.VMEM((PARTS, NZ, R, WIDE), F32),
    ]


def gather_tensor(buf, s1, r1, s2, r2, done):
    x, z, _, _ = place()
    low, high = pl.ds(0, NZ // 2), pl.ds(NZ // 2, NZ // 2)
    after, before = (x + 1) % NX, (x + 3) % NX
    up, down = {"tensor": after * NZ + z}, {"tensor": before * NZ + z}
    first, second = [], []
    for dz in Z_ORDER:
        ref = buf.at[x, z]
        first.append(
            rcopy(ref, ref, s1.at[dz], r1.at[dz], {"tensor": x * NZ + (z + dz) % NZ})
        )
        first[-1].start()

    def go(ref, i, dev):
        second.append(rcopy(ref, ref, s2.at[i], r2.at[i], dev))
        second[-1].start()

    yield
    arrive(first)
    go(buf.at[x, low], 0, up)
    go(buf.at[x, high], 1, down)
    go(buf.at[x, high], 2, up)
    go(buf.at[x, low], 3, down)
    yield
    second[0].wait_recv()
    go(buf.at[before, low], 4, up)
    second[1].wait_recv()
    go(buf.at[after, high], 5, down)
    yield
    arrive(second[2:])
    done += first + second


def rms(squares):
    return jnp.sqrt(squares / D + EPS)


class Refs(NamedTuple):
    hidden: object
    ids: object
    targets: object
    mask: object
    gain_h: object
    gain_e: object
    gain_f: object
    table_in: object
    proj_h_in: object
    proj_e_in: object
    head_in: object
    loss: object
    hidden_grad: object
    ph_grad: object
    pe_grad: object
    head_grad: object
    table: object
    proj_h: object
    proj_e: object
    head: object
    load_sems: object
    rms_all: object
    ids_all: object
    ids_col: object
    look: object
    look_recv: object
    nh: object
    ne: object
    unit: object
    fn: object
    logits: object
    core_recv: object
    y_recv: object
    lg: object
    flipped: object
    mg: object
    nhg: object
    nhg_recv: object
    sums: object
    part: object
    first: object
    near: object
    line: object
    last: object
    hidden_stats: object
    front_stats: object
    soft_stats: object
    last_stats: object
    masks: object
    losses: object
    squares: object
    inners: object
    ids_s: object
    ids_r: object
    emb_s: object
    emb_r: object
    hst_s: object
    hst_r: object
    fst_s: object
    fst_r: object
    rm_s: object
    rm_r: object
    gy_s: object
    gy_r: object
    gc_s: object
    gc_r: object
    mk_s: object
    mk_r: object
    red_s1: object
    red_r1: object
    red_s2: object
    red_r2: object
    sq_s: object
    sq_r: object
    agt_s1: object
    agt_r1: object
    agt_s2: object
    agt_r2: object
    co_s: object
    co_r: object
    ry_s: object
    ry_r: object
    st_s: object
    st_r: object
    lo_s: object
    lo_r: object
    ly_s: object
    ly_r: object
    lc_s: object
    lc_r: object
    ng_s: object
    ng_r: object
    ls_s: object
    ls_r: object


def kernel(*refs):
    k = Refs(*refs)
    x, z, c, y = place()
    t = x * NZ + z
    g = c * NY + y
    bar = greet_all()
    done = []
    loads = [
        pltpu.make_async_copy(src, dst, k.load_sems.at[i])
        for i, (src, dst) in enumerate(
            (
                (k.table_in, k.table),
                (k.proj_h_in, k.proj_h),
                (k.proj_e_in, k.proj_e),
                (k.head_in, k.head),
            )
        )
    ]
    for load in loads:
        load.start()
    hidden = k.hidden[...].astype(F32).T
    hidden_squares = jnp.sum(hidden * hidden, axis=1, keepdims=True)
    hidden_tile = to_tile([hidden_squares])
    pl.semaphore_wait(bar, NT - 1 + NG - 1)

    k.ids_all[g] = k.ids[...]
    sent_ids = share_g(k.ids_all, k.ids_s, k.ids_r)
    mask = k.mask[...].astype(F32)
    k.masks[g] = jnp.broadcast_to(mask, (8, OWN))
    sent_masks = share_g(k.masks, k.mk_s, k.mk_r)
    hidden_sent = share_tensor(hidden_tile, k.hidden_stats, k.hst_s, k.hst_r)
    arrive(sent_ids)
    done += sent_ids
    for b in range(NG):
        k.ids_col[pl.ds(b * OWN, OWN), :] = to_col(k.ids_all[b]) - g * TABLE

    loads[0].wait()
    step = 512

    def lookup(j, total):
        hits = k.ids_col[...] == lax.broadcasted_iota(jnp.int32, (1, step), 1) + j * step
        ones = jnp.where(hits, F32(1.0), F32(0.0)).astype(BF16)
        rows = k.table[:, pl.ds(pl.multiple_of(j * step, step), step)]
        return total + lax.dot_general(
            ones, rows, (((1,), (1,)), ((), ())), preferred_element_type=F32
        )

    total = lax.fori_loop(0, TABLE // step, lookup, jnp.zeros((NG * OWN, FEAT), F32))
    k.look[...] = total.astype(BF16).reshape(NG, OWN, FEAT)
    sent = scatter_g(k.look, k.look_recv, k.emb_s, k.emb_r)
    finish(hidden_sent)
    hidden_rms = rms(to_col(jnp.sum(k.hidden_stats[...], axis=0)[:1, :]))
    hidden_unit = hidden / hidden_rms
    k.sums[:, :FEAT] = hidden_unit
    k.sums[:, FEAT : FEAT + 1] = hidden_rms
    gain_h = k.gain_h[...].astype(F32)[None, :]
    gain_f = k.gain_f[...].astype(F32)[None, :]
    nh = (hidden_unit * gain_h).astype(BF16)
    k.nh[g // 2, pl.ds(g % 2 * 4, 4)] = nh.reshape(4, ROWS, FEAT)
    gather_nh = gather_g(k.nh, k.gy_s.at[0], k.gy_r.at[0], k.gc_s.at[0], k.gc_r.at[0], done)
    next(gather_nh)
    k.look_recv[g] = k.look[g]
    arrive(sent)
    done += sent
    embedded = k.look_recv[0].astype(F32)
    for b in range(1, NG):
        embedded = embedded + k.look_recv[b].astype(F32)
    embed_squares = jnp.sum(embedded * embedded, axis=1, keepdims=True)
    sent = share_tensor(to_tile([embed_squares]), k.front_stats, k.fst_s, k.fst_r)
    k.ne[g // 2, pl.ds(g % 2 * 4, 4)] = embedded.astype(BF16).reshape(4, ROWS, FEAT)
    gather_ne = gather_g(k.ne, k.gy_s.at[1], k.gy_r.at[1], k.gc_s.at[1], k.gc_r.at[1], done)
    next(gather_ne)
    next(gather_nh)
    finish(sent)
    embed_rms = rms(jnp.sum(k.front_stats[...], axis=0))
    k.rms_all[g] = embed_rms
    sent = share_g(k.rms_all, k.rm_s, k.rm_r)
    for one in (gather_ne, gather_nh, gather_ne, gather_nh, gather_ne):
        next(one, None)
    arrive(sent)
    done += sent
    gain_e = k.gain_e[...].astype(F32)[None, :]
    for one in done:
        one.wait_send()
    done = []
    for b in range(NG):
        raw = k.ne[b // 2, pl.ds(b % 2 * 4, 4)].reshape(OWN, FEAT).astype(F32)
        ne = (raw / to_col(k.rms_all[b][:1, :]) * gain_e).astype(BF16)
        k.ne[b // 2, pl.ds(b % 2 * 4, 4)] = ne.reshape(4, ROWS, FEAT)
    loads[1].wait()
    loads[2].wait()
    arrive(sent_masks)
    done += sent_masks
    mask_total = jnp.sum(k.masks[...][:, :1, :])
    weight = to_col(mask / mask_total)
    target = to_col(k.targets[...])
    mask = to_col(mask)

    def own_rows(array, p):
        return array.reshape(4, ROWS, array.shape[1])[:, p * R : (p + 1) * R].reshape(
            GR, array.shape[1]
        )

    def chain(p):
        bufs = [ref.at[p] for ref in (k.first, k.near, k.line, k.last)]
        part, fn, lg, mg = k.part.at[p], k.fn.at[p], k.lg.at[p], k.mg.at[p]
        logits, core_recv, y_recv = k.logits.at[p], k.core_recv.at[p], k.y_recv.at[p]
        rows = slice(p * R, (p + 1) * R)

        def sems(i):
            return [ref.at[p, i] for ref in (k.red_s1, k.red_r1, k.red_s2, k.red_r2)]

        def agt(i):
            return [ref.at[p, i] for ref in (k.agt_s1, k.agt_r1, k.agt_s2, k.agt_r2)]

        def project(xb):
            nh = k.nh[xb, :, rows, :].reshape(NZ * R, FEAT)
            ne = k.ne[xb, :, rows, :].reshape(NZ * R, FEAT)
            terms = jnp.dot(nh, k.proj_h[...], preferred_element_type=F32) + jnp.dot(
                ne, k.proj_e[...], preferred_element_type=F32
            )
            part[xb] = terms.reshape(NZ, R, WIDE)

        mixed = []
        steps = reduce_tensor(part, bufs + sems(0), project, done, mixed)
        next(steps)
        yield "rs1a"
        next(steps)
        yield "rs1x"
        next(steps)
        yield "rs1b"
        next(steps, None)
        mixed = mixed[0]
        own_squares = jnp.sum(mixed * mixed, axis=1, keepdims=True)
        k.squares[p, g] = jnp.broadcast_to(own_squares, (R, OWN))
        sent = share_g(k.squares.at[p], k.sq_s.at[p], k.sq_r.at[p])
        yield "sq"
        finish(sent)
        mixed_rms = rms(jnp.sum(k.squares[p], axis=0)[:, :1])
        mixed = mixed / mixed_rms
        k.unit[p] = mixed
        fn[x, z] = (mixed * gain_f).astype(BF16)
        steps = gather_tensor(fn, *agt(0), done)
        next(steps)
        yield "ag1"
        next(steps)
        yield "ag2"
        next(steps)
        yield "agx"
        next(steps, None)
        if p == 0:
            loads[3].wait()
        half = NY * GR
        other = 1 - c

        def product(core, n):
            out = jnp.dot(
                fn[pl.ds(core * 2, 2)].reshape(half, WIDE),
                k.head[:, n * CW : (n + 1) * CW],
                preferred_element_type=F32,
            )
            logits[core, :, :, n * CW : (n + 1) * CW] = out.reshape(NY, GR, CW)

        crossing, along = [], []
        for n in range(CHUNKS):
            product(other, n)
            columns = pl.ds(n * CW, CW)
            copy = rcopy(
                logits.at[other, :, :, columns],
                core_recv.at[:, :, columns],
                k.co_s.at[p, n],
                k.co_r.at[p, n],
                {"context": other},
            )
            copy.start()
            crossing.append(copy)
        after, far, before = ((y + dy) % NY for dy in (1, 2, 3))
        up, down = {"dp": after}, {"dp": before}

        def along_y(src, dst, i, dev):
            along.append(rcopy(src, dst, k.ry_s.at[p, i], k.ry_r.at[p, i], dev))
            along[-1].start()

        low, high = pl.ds(0, CW), pl.ds(CW, CW)
        for n, columns in enumerate((low, high)):
            product(c, n)
            crossing[n].wait_recv()
            logits[c, :, :, columns] = logits[c, :, :, columns] + core_recv[:, :, columns]
            far_to, near_to, slot, near = ((up, down, 1, before), (down, up, 0, after))[n]
            along_y(logits.at[c, far, :, columns], y_recv.at[2, :, columns], 2 * n, far_to)
            along_y(
                logits.at[c, near, :, columns], y_recv.at[slot, :, columns], 2 * n + 1, near_to
            )
        flipped = k.flipped.at[p]
        for xb in range(NX):
            block = NZ * R
            flipped[:, xb * block : (xb + 1) * block] = fn[xb].reshape(block, WIDE).T
        yield "ry"
        along[0].wait_recv()
        logits[c, after, :, low] = logits[c, after, :, low] + y_recv[2, :, low]
        along_y(logits.at[c, after, :, low], y_recv.at[0, :, low], 4, up)
        along[2].wait_recv()
        logits[c, before, :, high] = logits[c, before, :, high] + y_recv[2, :, high]
        along_y(logits.at[c, before, :, high], y_recv.at[1, :, high], 5, down)
        yield "ryx"
        arrive([along[1], along[3], along[4], along[5]])
        done.extend(along + crossing)
        own = logits[c, y] + y_recv[0] + y_recv[1]
        logits[c, y] = own
        columns = lax.broadcasted_iota(jnp.int32, (1, VOC), 1) + t * VOC
        hits = columns == own_rows(target, p)
        top = jnp.max(own, axis=1, keepdims=True)
        total = jnp.sum(jnp.exp(own - top), axis=1, keepdims=True)
        picked = jnp.sum(jnp.where(hits, own, F32(0.0)), axis=1, keepdims=True)
        sent = share_tensor(
            to_tile([top, total, picked]), k.soft_stats.at[p], k.st_s.at[p], k.st_r.at[p]
        )
        yield "st"
        finish(sent)
        every = k.soft_stats[p]
        tops = every[:, 0, :]
        row_top = jnp.max(tops, axis=0, keepdims=True)
        exp_total = jnp.sum(every[:, 1, :] * jnp.exp(tops - row_top), axis=0, keepdims=True)
        picked = to_col(jnp.sum(every[:, 2, :], axis=0, keepdims=True), GR)
        log_total = to_col(row_top + jnp.log(exp_total), GR)
        own = logits[c, y]
        probs = jnp.exp(own - log_total)
        grads = own_rows(weight, p) * (probs - jnp.where(hits, F32(1.0), F32(0.0)))
        lg[g // 2, pl.ds(g % 2 * 4, 4)] = grads.astype(BF16).reshape(4, R, VOC)
        steps = gather_g(lg, k.ly_s.at[p], k.ly_r.at[p], k.lc_s.at[p], k.lc_r.at[p], done)
        next(steps)
        k.losses[p, g] = jnp.broadcast_to(
            jnp.sum(own_rows(mask, p) * (log_total - picked), axis=0, keepdims=True), (8, OWN)
        )
        done.extend(share_g(k.losses.at[p], k.lo_s.at[p], k.lo_r.at[p]))
        yield "lg"
        next(steps)
        yield "lgf"
        next(steps)
        yield "lgc"
        next(steps, None)

        def terms(xb):
            out = lax.dot_general(
                lg[xb].reshape(NZ * R, VOC),
                k.head[...],
                (((1,), (1,)), ((), ())),
                preferred_element_type=F32,
            )
            part[xb] = out.reshape(NZ, R, WIDE)

        final = []
        steps = reduce_tensor(part, bufs + sems(1), terms, done, final)
        next(steps)
        yield "r2a"
        next(steps)
        yield "r2x"
        next(steps)
        yield "r2b"
        next(steps, None)
        scaled = final[0] * gain_f
        unit = k.unit[p]
        own_inner = jnp.sum(scaled * unit, axis=1, keepdims=True)
        k.inners[p, g] = jnp.broadcast_to(own_inner, (R, OWN))
        sent = share_g(k.inners.at[p], k.sq_s.at[PARTS + p], k.sq_r.at[PARTS + p])
        yield "in"
        finish(sent)
        inner = jnp.sum(k.inners[p], axis=0)[:, :1] / D
        mg[x, z] = ((scaled - unit * inner) / mixed_rms).astype(BF16)
        steps = gather_tensor(mg, *agt(1), done)
        next(steps)
        yield "mg1"
        next(steps)
        yield "mg2"
        next(steps)
        yield "mgx"
        next(steps, None)
        nhg = k.nhg.at[p]
        nhg[...] = lax.dot_general(
            mg[...].reshape(TOK, WIDE),
            k.proj_h[...],
            (((1,), (1,)), ((), ())),
            preferred_element_type=F32,
        ).reshape(NG, GR, FEAT)
        sent = scatter_g(nhg, k.nhg_recv.at[p], k.ng_s.at[p], k.ng_r.at[p])
        k.nhg_recv[p, g] = nhg[g]
        yield "ng"
        arrive(sent)
        done.extend(sent)
        scaled = jnp.sum(k.nhg_recv[p], axis=0) * gain_h
        unit_rows = own_rows(k.sums[:, :FEAT], p)
        inner = jnp.sum(scaled * unit_rows, axis=1, keepdims=True)
        sent = share_tensor(
            to_tile([inner]), k.last_stats.at[p], k.ls_s.at[p], k.ls_r.at[p]
        )
        yield "ls"
        finish(sent)
        inner = to_col(jnp.sum(k.last_stats[p], axis=0)[:1, :], GR) / D
        hidden_grad = (scaled - unit_rows * inner) / own_rows(k.sums[:, FEAT : FEAT + 1], p)
        k.nhg_recv[p, 0] = hidden_grad

    def head_side():
        def tile(n, carry):
            columns = pl.ds(pl.multiple_of(n * 256, 256), 256)
            total = jnp.zeros((WIDE, 256), F32)
            for p in range(PARTS):
                total = total + jnp.dot(
                    k.flipped[p],
                    k.lg[p, :, :, :, columns].reshape(TOK, 256),
                    preferred_element_type=F32,
                )
            k.head_grad[:, columns] = total.astype(BF16)
            return carry

        lax.fori_loop(0, VOC // 256, tile, 0)
        yield

    def proj_side():
        for ref, out in ((k.nh, k.ph_grad), (k.ne, k.pe_grad)):
            total = jnp.zeros((FEAT, WIDE), F32)
            for p in range(PARTS):
                rows = ref[:, :, p * R : (p + 1) * R, :].reshape(TOK, FEAT)
                total = total + lax.dot_general(
                    rows,
                    k.mg[p].reshape(TOK, WIDE),
                    (((0,), (0,)), ((), ())),
                    preferred_element_type=F32,
                )
            out[...] = total.astype(BF16)
        yield

    flows = {"a": chain(0), "b": chain(1), "h": head_side(), "p": proj_side()}
    for step in SCHEDULE:
        name, label = step.split(".")
        for reached in flows[name]:
            if reached == label:
                break
    for one in done:
        one.wait_send()
    for p in range(PARTS):
        for i, (_, dev) in enumerate(g_peers()):
            rcopy(
                k.losses.at[p, g], k.losses.at[p, g], k.lo_s.at[p, i], k.lo_r.at[p, i], dev
            ).wait_recv()
    loss = k.losses[0]
    for p in range(1, PARTS):
        loss = loss + k.losses[p]
    k.loss[...] = jnp.sum(loss, axis=0)[:1, :1] / mask_total
    whole = jnp.concatenate(
        [k.nhg_recv[p, 0].reshape(4, R, FEAT) for p in range(PARTS)], axis=1
    ).reshape(OWN, FEAT)
    k.hidden_grad[...] = whole.T.astype(BF16)


SCHEDULE = (
    "a.rs1a",
    "a.rs1x",
    "b.rs1a",
    "a.rs1b",
    "b.rs1x",
    "a.sq",
    "b.rs1b",
    "a.ag1",
    "a.ag2",
    "b.sq",
    "a.agx",
    "b.ag1",
    "a.ry",
    "b.ag2",
    "b.agx",
    "a.ryx",
    "b.ry",
    "a.st",
    "b.ryx",
    "a.lg",
    "a.lgf",
    "b.st",
    "a.lgc",
    "b.lg",
    "a.r2a",
    "b.lgf",
    "a.r2x",
    "b.lgc",
    "a.r2b",
    "b.r2a",
    "h.end",
    "a.in",
    "b.r2x",
    "a.mg1",
    "a.mg2",
    "b.r2b",
    "a.mgx",
    "b.in",
    "b.mg1",
    "a.ng",
    "b.mg2",
    "b.mgx",
    "a.ls",
    "b.ng",
    "p.end",
    "b.ls",
    "a.end",
    "b.end",
)


def vmem(n):
    return [pl.BlockSpec(memory_space=pltpu.VMEM)] * n


def dma(*shape):
    return pltpu.SemaphoreType.DMA(shape)


def pairs(*shapes):
    return [dma(*shape) for shape in shapes for _ in range(2)]


def call(*args):
    return pl.pallas_call(
        kernel,
        out_shape=(
            jax.ShapeDtypeStruct((1, 1), F32),
            jax.ShapeDtypeStruct((FEAT, OWN), BF16),
            jax.ShapeDtypeStruct((FEAT, WIDE), BF16),
            jax.ShapeDtypeStruct((FEAT, WIDE), BF16),
            jax.ShapeDtypeStruct((WIDE, VOC), BF16),
        ),
        in_specs=vmem(7) + [pl.BlockSpec(memory_space=pl.ANY)] * 4,
        out_specs=tuple(vmem(5)),
        scratch_shapes=[
            pltpu.VMEM((FEAT, TABLE), BF16),
            pltpu.VMEM((FEAT, WIDE), BF16),
            pltpu.VMEM((FEAT, WIDE), BF16),
            pltpu.VMEM((WIDE, VOC), BF16),
            dma(4),
            pltpu.VMEM((NG, 8, OWN), F32),
            pltpu.VMEM((NG, 1, OWN), jnp.int32),
            pltpu.VMEM((NG * OWN, 1), jnp.int32),
            pltpu.VMEM((NG, OWN, FEAT), BF16),
            pltpu.VMEM((NG, OWN, FEAT), BF16),
            pltpu.VMEM((NX, NZ, ROWS, FEAT), BF16),
            pltpu.VMEM((NX, NZ, ROWS, FEAT), BF16),
            pltpu.VMEM((PARTS, R, WIDE), F32),
            pltpu.VMEM((PARTS, NX, NZ, R, WIDE), BF16),
            pltpu.VMEM((PARTS, NC, NY, GR, VOC), F32),
            pltpu.VMEM((PARTS, NY, GR, VOC), F32),
            pltpu.VMEM((PARTS, NY - 1, GR, VOC), F32),
            pltpu.VMEM((PARTS, NX, NZ, R, VOC), BF16),
            pltpu.VMEM((PARTS, WIDE, TOK), BF16),
            pltpu.VMEM((PARTS, NX, NZ, R, WIDE), BF16),
            pltpu.VMEM((PARTS, NG, GR, FEAT), F32),
            pltpu.VMEM((PARTS, NG, GR, FEAT), F32),
            pltpu.VMEM((OWN, 256), F32),
        ]
        + reduce_scratch()
        + [
            pltpu.VMEM((NT, 8, OWN), F32),
            pltpu.VMEM((NT, 8, OWN), F32),
            pltpu.VMEM((PARTS, NT, 8, OWN), F32),
            pltpu.VMEM((PARTS, NT, 8, OWN), F32),
            pltpu.VMEM((NG, 8, OWN), F32),
            pltpu.VMEM((PARTS, NG, 8, OWN), F32),
            pltpu.VMEM((PARTS, NG, R, OWN), F32),
            pltpu.VMEM((PARTS, NG, R, OWN), F32),
        ]
        + pairs((NG - 1,), (NG - 1,))
        + [pltpu.SemaphoreType.DMA] * 4
        + pairs((NG - 1,), (2, 4), (2, 4), (NG - 1,))
        + pairs((PARTS, 2, NZ), (PARTS, 2, NZ), (2 * PARTS, NG - 1))
        + pairs((PARTS, 2, NZ), (PARTS, 2, NZ))
        + pairs((PARTS, CHUNKS), (PARTS, 6), (PARTS,), (PARTS, NG - 1))
        + pairs((PARTS, 4), (PARTS, 4), (PARTS, NG - 1), (PARTS,)),
        compiler_params=pltpu.CompilerParams(
            collective_id=0, has_side_effects=True, vmem_limit_bytes=VMEM_LIMIT
        ),
        name="whole",
    )(*args)


def settle_kernel(a, b, c, d, a_out, b_out, c_out, d_out):
    @pl.when(pl.program_id(0) == 0)
    def _():
        a_out[...] = a[...]
        b_out[...] = b[...]
        c_out[...] = c[...]

    d_out[...] = d[...]


def settle(*arrays):
    blocks = 4
    specs = [pl.BlockSpec(a.shape, lambda i: (0, 0)) for a in arrays[:3]]
    specs.append(pl.BlockSpec((WIDE // blocks, VOC), lambda i: (i, 0)))
    return pl.pallas_call(
        settle_kernel,
        grid=(blocks,),
        out_shape=tuple(jax.ShapeDtypeStruct(a.shape, a.dtype) for a in arrays),
        in_specs=specs,
        out_specs=tuple(specs),
        compiler_params=pltpu.CompilerParams(vmem_limit_bytes=VMEM_LIMIT),
        name="settle",
    )(*arrays)


def per_device(
    hidden_prev,
    next_ids,
    targets,
    loss_mask,
    gain_hidden,
    gain_embed,
    gain_final,
    embed_table,
    proj_hidden,
    proj_embed,
    head_weight,
):
    loss, hidden_grad, ph_grad, pe_grad, head_grad = call(
        hidden_prev.T,
        next_ids[None, :],
        targets[None, :],
        loss_mask[None, :],
        gain_hidden,
        gain_embed,
        gain_final,
        embed_table.T,
        proj_hidden,
        proj_embed,
        head_weight,
    )
    hidden_grad, ph_grad, pe_grad, head_grad = settle(hidden_grad, ph_grad, pe_grad, head_grad)
    return (loss[0, 0], hidden_grad.T, ph_grad, pe_grad, head_grad)


def solution(mesh):
    return jax.shard_map(
        per_device,
        mesh=mesh,
        in_specs=(
            P(("context", "dp"), "tensor"),
            P(("context", "dp")),
            P(("context", "dp")),
            P(("context", "dp")),
            P("tensor"),
            P("tensor"),
            P(("context", "dp")),
            P(("context", "dp"), "tensor"),
            P("tensor", ("context", "dp")),
            P("tensor", ("context", "dp")),
            P(("context", "dp"), "tensor"),
        ),
        out_specs=(
            P(),
            P(("context", "dp"), "tensor"),
            P("tensor", ("context", "dp")),
            P("tensor", ("context", "dp")),
            P(("context", "dp"), "tensor"),
        ),
        check_vma=False,
    )
```

```python
from typing import NamedTuple

import jax
import jax.numpy as jnp
from jax import lax
from jax.experimental import pallas as pl
from jax.experimental.pallas import tpu as pltpu
from jax.sharding import PartitionSpec as P

D = 7168
EPS = 1e-06
MESH = pl.DeviceIdType.MESH
F32 = jnp.float32
BF16 = jnp.bfloat16
NX, NZ, NC, NY = 4, 8, 2, 4
NT, NG = NX * NZ, NC * NY
ROWS = 32
OWN = 128
WIDE = 896
FEAT = 224
VOC = 2048
TABLE = 8192
Z_ORDER = (4, 3, 5, 2, 6, 1, 7)
VMEM_LIMIT = 62 * 1024 * 1024
PARTS = 2
R = ROWS // PARTS
TOK = NX * NZ * R
GR = OWN // PARTS
CHUNKS = 2
CW = VOC // CHUNKS


def place():
    t = lax.axis_index("tensor")
    return t // NZ, t % NZ, lax.axis_index("context"), lax.axis_index("dp")


def rcopy(src, dst, ss, rs, dev):
    return pltpu.make_async_remote_copy(
        src_ref=src, dst_ref=dst, send_sem=ss, recv_sem=rs, device_id=dev, device_id_type=MESH
    )


def greet_all():
    x, z, c, y = place()
    t = x * NZ + z
    bar = pltpu.get_barrier_semaphore()

    def hello(k, carry):
        pl.semaphore_signal(
            bar, inc=1, device_id={"tensor": (t + k) % NT}, device_id_type=MESH
        )
        return carry

    lax.fori_loop(1, NT, hello, 0)
    for dc in range(NC):
        for dy in range(NY):
            if dc or dy:
                pl.semaphore_signal(
                    bar,
                    inc=1,
                    device_id={"context": (c + dc) % NC, "dp": (y + dy) % NY},
                    device_id_type=MESH,
                )
    return bar


def to_tile(columns):
    n = columns[0].shape[0]
    lane = lax.broadcasted_iota(jnp.int32, (n, OWN), 1)
    wide = jnp.zeros((n, OWN), F32)
    for i, column in enumerate(columns):
        wide = jnp.where(lane == i, column, wide)
    if n < OWN:
        wide = jnp.concatenate([wide] * (OWN // n), axis=0)
    return wide.T[:8, :]


def to_col(row, n=OWN):
    return jnp.broadcast_to(row, (OWN, OWN)).T[:n, :1]


def share_tensor(tile, recv, ss, rs):
    x, z, _, _ = place()
    t = x * NZ + z
    recv[t] = tile

    def send(k, carry):
        rcopy(recv.at[t], recv.at[t], ss, rs, {"tensor": (t + k) % NT}).start()
        return carry

    lax.fori_loop(1, NT, send, 0)
    return [
        rcopy(
            recv.at[pl.ds(0, NT - 1)], recv.at[pl.ds(0, NT - 1)], ss, rs, {"tensor": (t + 1) % NT}
        )
    ]


def g_peers():
    _, _, c, y = place()
    for dy in (2, 1, 3, 0):
        for dc in (1, 0):
            if dc or dy:
                cb, yb = (c + dc) % NC, (y + dy) % NY
                yield cb * NY + yb, {"context": cb, "dp": yb}


def share_g(recv, ss, rs):
    _, _, c, y = place()
    g = c * NY + y
    copies = []
    for i, (_, dev) in enumerate(g_peers()):
        copy = rcopy(recv.at[g], recv.at[g], ss.at[i], rs.at[i], dev)
        copy.start()
        copies.append(copy)
    return copies


def scatter_g(src, recv, ss, rs):
    _, _, c, y = place()
    g = c * NY + y
    copies = []
    for i, (gb, dev) in enumerate(g_peers()):
        copy = rcopy(src.at[gb], recv.at[g], ss.at[i], rs.at[i], dev)
        copy.start()
        copies.append(copy)
    return copies


def arrive(copies):
    for copy in copies:
        copy.wait_recv()


def finish(copies):
    for copy in copies:
        copy.wait()


def g_block(ref, g):
    return ref.at[g // 2, pl.ds(g % 2 * 4, 4)]


def gather_g(buf, ssy, rsy, ssc, rsc, done):
    _, _, c, y = place()
    own, near = (c * NY + (y + dy) % NY for dy in (0, 1))
    before, far = (c * NY + (y + dy) % NY for dy in (3, 2))
    copies, ahead = [], []

    def go(ref, i, dev):
        copies.append(rcopy(ref, ref, ssy.at[i], rsy.at[i], dev))
        copies[-1].start()

    def cross(block, i):
        ref = g_block(buf, block)
        ahead.append(rcopy(ref, ref, ssc.at[i], rsc.at[i], {"context": 1 - c}))
        ahead[-1].start()

    up, down = {"dp": (y + 1) % NY}, {"dp": (y + 3) % NY}
    go(g_block(buf, own), 0, up)
    go(g_block(buf, own), 1, down)
    cross(own, 0)
    yield
    copies[0].wait_recv()
    go(g_block(buf, before).at[pl.ds(0, 2)], 2, up)
    cross(before, 1)
    copies[1].wait_recv()
    go(g_block(buf, near).at[pl.ds(2, 2)], 3, down)
    cross(near, 2)
    yield
    copies[2].wait_recv()
    copies[3].wait_recv()
    cross(far, 3)
    yield
    arrive(ahead)
    done += ahead + copies


def reduce_tensor(part, bufs, compute_block, done, result):
    first, near, line, last, s1, r1, s2, r2 = bufs
    x, z, _, _ = place()
    low, high = pl.ds(0, NZ // 2), pl.ds(NZ // 2, NZ // 2)
    after, far, before = ((x + dx) % NX for dx in (1, 2, 3))
    up, down = {"tensor": after * NZ + z}, {"tensor": before * NZ + z}
    copies = []

    def go(src, dst, i, dev):
        copies.append(rcopy(src, dst, s1.at[i], r1.at[i], dev))
        copies[-1].start()

    compute_block(far)
    go(part.at[far, low], first.at[0], 0, up)
    go(part.at[far, high], first.at[1], 1, down)
    compute_block(after)
    go(part.at[after, high], near.at[0, high], 2, up)
    compute_block(before)
    go(part.at[before, low], near.at[1, low], 3, down)
    compute_block(x)
    yield
    copies[0].wait_recv()
    part[after, low] = part[after, low] + first[0]
    go(part.at[after, low], near.at[0, low], 4, up)
    copies[1].wait_recv()
    part[before, high] = part[before, high] + first[1]
    go(part.at[before, high], near.at[1, high], 5, down)
    yield
    arrive(copies[2:])
    second = []
    for dz in Z_ORDER + (0,):
        zb = (z + dz) % NZ
        line[zb] = part[x, zb] + near[0, zb] + near[1, zb]
        if dz:
            second.append(
                rcopy(line.at[zb], last.at[z], s2.at[dz], r2.at[dz], {"tensor": x * NZ + zb})
            )
            second[-1].start()
    yield
    arrive(second)
    total = line[z]
    for dz in Z_ORDER:
        total = total + last[(z + NZ - dz) % NZ]
    for copy in copies + second:
        copy.wait_send()
    result.append(total)


def reduce_scratch():
    return [
        pltpu.VMEM((PARTS, NX, NZ, R, WIDE), F32),
        pltpu.VMEM((PARTS, 2, NZ // 2, R, WIDE), F32),
        pltpu.VMEM((PARTS, 2, NZ, R, WIDE), F32),
        pltpu.VMEM((PARTS, NZ, R, WIDE), F32),
        pltpu.VMEM((PARTS, NZ, R, WIDE), F32),
    ]


def gather_tensor(buf, s1, r1, s2, r2, done):
    x, z, _, _ = place()
    low, high = pl.ds(0, NZ // 2), pl.ds(NZ // 2, NZ // 2)
    after, before = (x + 1) % NX, (x + 3) % NX
    up, down = {"tensor": after * NZ + z}, {"tensor": before * NZ + z}
    first, second = [], []
    for dz in Z_ORDER:
        ref = buf.at[x, z]
        first.append(
            rcopy(ref, ref, s1.at[dz], r1.at[dz], {"tensor": x * NZ + (z + dz) % NZ})
        )
        first[-1].start()

    def go(ref, i, dev):
        second.append(rcopy(ref, ref, s2.at[i], r2.at[i], dev))
        second[-1].start()

    yield
    arrive(first)
    go(buf.at[x, low], 0, up)
    go(buf.at[x, high], 1, down)
    go(buf.at[x, high], 2, up)
    go(buf.at[x, low], 3, down)
    yield
    second[0].wait_recv()
    go(buf.at[before, low], 4, up)
    second[1].wait_recv()
    go(buf.at[after, high], 5, down)
    yield
    arrive(second[2:])
    done += first + second


def rms(squares):
    return jnp.sqrt(squares / D + EPS)


class Refs(NamedTuple):
    hidden: object
    ids: object
    targets: object
    mask: object
    gain_h: object
    gain_e: object
    gain_f: object
    table_in: object
    proj_h_in: object
    proj_e_in: object
    head_in: object
    loss: object
    hidden_grad: object
    ph_grad: object
    pe_grad: object
    head_grad: object
    table: object
    proj_h: object
    proj_e: object
    head: object
    load_sems: object
    rms_all: object
    ids_all: object
    ids_col: object
    look: object
    look_recv: object
    nh: object
    ne: object
    unit: object
    fn: object
    logits: object
    core_recv: object
    y_recv: object
    lg: object
    flipped: object
    mg: object
    nhg: object
    nhg_recv: object
    sums: object
    part: object
    first: object
    near: object
    line: object
    last: object
    hidden_stats: object
    front_stats: object
    soft_stats: object
    last_stats: object
    masks: object
    losses: object
    squares: object
    inners: object
    ids_s: object
    ids_r: object
    emb_s: object
    emb_r: object
    hst_s: object
    hst_r: object
    fst_s: object
    fst_r: object
    rm_s: object
    rm_r: object
    gy_s: object
    gy_r: object
    gc_s: object
    gc_r: object
    mk_s: object
    mk_r: object
    red_s1: object
    red_r1: object
    red_s2: object
    red_r2: object
    sq_s: object
    sq_r: object
    agt_s1: object
    agt_r1: object
    agt_s2: object
    agt_r2: object
    co_s: object
    co_r: object
    ry_s: object
    ry_r: object
    st_s: object
    st_r: object
    lo_s: object
    lo_r: object
    ly_s: object
    ly_r: object
    lc_s: object
    lc_r: object
    ng_s: object
    ng_r: object
    ls_s: object
    ls_r: object


def kernel(*refs):
    k = Refs(*refs)
    x, z, c, y = place()
    t = x * NZ + z
    g = c * NY + y
    bar = greet_all()
    done = []
    loads = [
        pltpu.make_async_copy(src, dst, k.load_sems.at[i])
        for i, (src, dst) in enumerate(
            (
                (k.table_in, k.table),
                (k.proj_h_in, k.proj_h),
                (k.proj_e_in, k.proj_e),
                (k.head_in, k.head),
            )
        )
    ]
    for load in loads:
        load.start()
    hidden = k.hidden[...].astype(F32).T
    hidden_squares = jnp.sum(hidden * hidden, axis=1, keepdims=True)
    hidden_tile = to_tile([hidden_squares])
    pl.semaphore_wait(bar, NT - 1 + NG - 1)

    k.ids_all[g] = k.ids[...]
    sent_ids = share_g(k.ids_all, k.ids_s, k.ids_r)
    mask = k.mask[...].astype(F32)
    k.masks[g] = jnp.broadcast_to(mask, (8, OWN))
    sent_masks = share_g(k.masks, k.mk_s, k.mk_r)
    hidden_sent = share_tensor(hidden_tile, k.hidden_stats, k.hst_s, k.hst_r)
    arrive(sent_ids)
    done += sent_ids
    for b in range(NG):
        k.ids_col[pl.ds(b * OWN, OWN), :] = to_col(k.ids_all[b]) - g * TABLE

    loads[0].wait()
    step = 512

    def lookup(j, total):
        hits = k.ids_col[...] == lax.broadcasted_iota(jnp.int32, (1, step), 1) + j * step
        ones = jnp.where(hits, F32(1.0), F32(0.0)).astype(BF16)
        rows = k.table[:, pl.ds(pl.multiple_of(j * step, step), step)]
        return total + lax.dot_general(
            ones, rows, (((1,), (1,)), ((), ())), preferred_element_type=F32
        )

    total = lax.fori_loop(0, TABLE // step, lookup, jnp.zeros((NG * OWN, FEAT), F32))
    k.look[...] = total.astype(BF16).reshape(NG, OWN, FEAT)
    sent = scatter_g(k.look, k.look_recv, k.emb_s, k.emb_r)
    finish(hidden_sent)
    hidden_rms = rms(to_col(jnp.sum(k.hidden_stats[...], axis=0)[:1, :]))
    hidden_unit = hidden / hidden_rms
    k.sums[:, :FEAT] = hidden_unit
    k.sums[:, FEAT : FEAT + 1] = hidden_rms
    gain_h = k.gain_h[...].astype(F32)[None, :]
    gain_f = k.gain_f[...].astype(F32)[None, :]
    nh = (hidden_unit * gain_h).astype(BF16)
    k.nh[g // 2, pl.ds(g % 2 * 4, 4)] = nh.reshape(4, ROWS, FEAT)
    gather_nh = gather_g(k.nh, k.gy_s.at[0], k.gy_r.at[0], k.gc_s.at[0], k.gc_r.at[0], done)
    next(gather_nh)
    k.look_recv[g] = k.look[g]
    arrive(sent)
    done += sent
    embedded = k.look_recv[0].astype(F32)
    for b in range(1, NG):
        embedded = embedded + k.look_recv[b].astype(F32)
    embed_squares = jnp.sum(embedded * embedded, axis=1, keepdims=True)
    sent = share_tensor(to_tile([embed_squares]), k.front_stats, k.fst_s, k.fst_r)
    k.ne[g // 2, pl.ds(g % 2 * 4, 4)] = embedded.astype(BF16).reshape(4, ROWS, FEAT)
    gather_ne = gather_g(k.ne, k.gy_s.at[1], k.gy_r.at[1], k.gc_s.at[1], k.gc_r.at[1], done)
    next(gather_ne)
    next(gather_nh)
    finish(sent)
    embed_rms = rms(jnp.sum(k.front_stats[...], axis=0))
    k.rms_all[g] = embed_rms
    sent = share_g(k.rms_all, k.rm_s, k.rm_r)
    for one in (gather_ne, gather_nh, gather_ne, gather_nh, gather_ne):
        next(one, None)
    arrive(sent)
    done += sent
    gain_e = k.gain_e[...].astype(F32)[None, :]
    for one in done:
        one.wait_send()
    done = []
    for b in range(NG):
        raw = k.ne[b // 2, pl.ds(b % 2 * 4, 4)].reshape(OWN, FEAT).astype(F32)
        ne = (raw / to_col(k.rms_all[b][:1, :]) * gain_e).astype(BF16)
        k.ne[b // 2, pl.ds(b % 2 * 4, 4)] = ne.reshape(4, ROWS, FEAT)
    loads[1].wait()
    loads[2].wait()
    arrive(sent_masks)
    done += sent_masks
    mask_total = jnp.sum(k.masks[...][:, :1, :])
    weight = to_col(mask / mask_total)
    target = to_col(k.targets[...])
    mask = to_col(mask)

    def own_rows(array, p):
        return array.reshape(4, ROWS, array.shape[1])[:, p * R : (p + 1) * R].reshape(
            GR, array.shape[1]
        )

    def chain(p):
        bufs = [ref.at[p] for ref in (k.first, k.near, k.line, k.last)]
        part, fn, lg, mg = k.part.at[p], k.fn.at[p], k.lg.at[p], k.mg.at[p]
        logits, core_recv, y_recv = k.logits.at[p], k.core_recv.at[p], k.y_recv.at[p]
        rows = slice(p * R, (p + 1) * R)

        def sems(i):
            return [ref.at[p, i] for ref in (k.red_s1, k.red_r1, k.red_s2, k.red_r2)]

        def agt(i):
            return [ref.at[p, i] for ref in (k.agt_s1, k.agt_r1, k.agt_s2, k.agt_r2)]

        def project(xb):
            nh = k.nh[xb, :, rows, :].reshape(NZ * R, FEAT)
            ne = k.ne[xb, :, rows, :].reshape(NZ * R, FEAT)
            terms = jnp.dot(nh, k.proj_h[...], preferred_element_type=F32) + jnp.dot(
                ne, k.proj_e[...], preferred_element_type=F32
            )
            part[xb] = terms.reshape(NZ, R, WIDE)

        mixed = []
        steps = reduce_tensor(part, bufs + sems(0), project, done, mixed)
        next(steps)
        yield "rs1a"
        next(steps)
        yield "rs1x"
        next(steps)
        yield "rs1b"
        next(steps, None)
        mixed = mixed[0]
        own_squares = jnp.sum(mixed * mixed, axis=1, keepdims=True)
        k.squares[p, g] = jnp.broadcast_to(own_squares, (R, OWN))
        sent = share_g(k.squares.at[p], k.sq_s.at[p], k.sq_r.at[p])
        yield "sq"
        finish(sent)
        mixed_rms = rms(jnp.sum(k.squares[p], axis=0)[:, :1])
        mixed = mixed / mixed_rms
        k.unit[p] = mixed
        fn[x, z] = (mixed * gain_f).astype(BF16)
        steps = gather_tensor(fn, *agt(0), done)
        next(steps)
        yield "ag1"
        next(steps)
        yield "ag2"
        next(steps)
        yield "agx"
        next(steps, None)
        if p == 0:
            loads[3].wait()
        half = NY * GR
        other = 1 - c

        def product(core, n):
            out = jnp.dot(
                fn[pl.ds(core * 2, 2)].reshape(half, WIDE),
                k.head[:, n * CW : (n + 1) * CW],
                preferred_element_type=F32,
            )
            logits[core, :, :, n * CW : (n + 1) * CW] = out.reshape(NY, GR, CW)

        crossing, along = [], []
        for n in range(CHUNKS):
            product(other, n)
            columns = pl.ds(n * CW, CW)
            copy = rcopy(
                logits.at[other, :, :, columns],
                core_recv.at[:, :, columns],
                k.co_s.at[p, n],
                k.co_r.at[p, n],
                {"context": other},
            )
            copy.start()
            crossing.append(copy)
        after, far, before = ((y + dy) % NY for dy in (1, 2, 3))
        up, down = {"dp": after}, {"dp": before}

        def along_y(src, dst, i, dev):
            along.append(rcopy(src, dst, k.ry_s.at[p, i], k.ry_r.at[p, i], dev))
            along[-1].start()

        low, high = pl.ds(0, CW), pl.ds(CW, CW)
        for n, columns in enumerate((low, high)):
            product(c, n)
            crossing[n].wait_recv()
            logits[c, :, :, columns] = logits[c, :, :, columns] + core_recv[:, :, columns]
            far_to, near_to, slot, near = ((up, down, 1, before), (down, up, 0, after))[n]
            along_y(logits.at[c, far, :, columns], y_recv.at[2, :, columns], 2 * n, far_to)
            along_y(
                logits.at[c, near, :, columns], y_recv.at[slot, :, columns], 2 * n + 1, near_to
            )
        flipped = k.flipped.at[p]
        for xb in range(NX):
            block = NZ * R
            flipped[:, xb * block : (xb + 1) * block] = fn[xb].reshape(block, WIDE).T
        yield "ry"
        along[0].wait_recv()
        logits[c, after, :, low] = logits[c, after, :, low] + y_recv[2, :, low]
        along_y(logits.at[c, after, :, low], y_recv.at[0, :, low], 4, up)
        along[2].wait_recv()
        logits[c, before, :, high] = logits[c, before, :, high] + y_recv[2, :, high]
        along_y(logits.at[c, before, :, high], y_recv.at[1, :, high], 5, down)
        yield "ryx"
        arrive([along[1], along[3], along[4], along[5]])
        done.extend(along + crossing)
        own = logits[c, y] + y_recv[0] + y_recv[1]
        logits[c, y] = own
        columns = lax.broadcasted_iota(jnp.int32, (1, VOC), 1) + t * VOC
        hits = columns == own_rows(target, p)
        top = jnp.max(own, axis=1, keepdims=True)
        total = jnp.sum(jnp.exp(own - top), axis=1, keepdims=True)
        picked = jnp.sum(jnp.where(hits, own, F32(0.0)), axis=1, keepdims=True)
        sent = share_tensor(
            to_tile([top, total, picked]), k.soft_stats.at[p], k.st_s.at[p], k.st_r.at[p]
        )
        yield "st"
        finish(sent)
        every = k.soft_stats[p]
        tops = every[:, 0, :]
        row_top = jnp.max(tops, axis=0, keepdims=True)
        exp_total = jnp.sum(every[:, 1, :] * jnp.exp(tops - row_top), axis=0, keepdims=True)
        picked = to_col(jnp.sum(every[:, 2, :], axis=0, keepdims=True), GR)
        log_total = to_col(row_top + jnp.log(exp_total), GR)
        own = logits[c, y]
        probs = jnp.exp(own - log_total)
        grads = own_rows(weight, p) * (probs - jnp.where(hits, F32(1.0), F32(0.0)))
        lg[g // 2, pl.ds(g % 2 * 4, 4)] = grads.astype(BF16).reshape(4, R, VOC)
        steps = gather_g(lg, k.ly_s.at[p], k.ly_r.at[p], k.lc_s.at[p], k.lc_r.at[p], done)
        next(steps)
        k.losses[p, g] = jnp.broadcast_to(
            jnp.sum(own_rows(mask, p) * (log_total - picked), axis=0, keepdims=True), (8, OWN)
        )
        done.extend(share_g(k.losses.at[p], k.lo_s.at[p], k.lo_r.at[p]))
        yield "lg"
        next(steps)
        yield "lgf"
        next(steps)
        yield "lgc"
        next(steps, None)

        def terms(xb):
            out = lax.dot_general(
                lg[xb].reshape(NZ * R, VOC),
                k.head[...],
                (((1,), (1,)), ((), ())),
                preferred_element_type=F32,
            )
            part[xb] = out.reshape(NZ, R, WIDE)

        final = []
        steps = reduce_tensor(part, bufs + sems(1), terms, done, final)
        next(steps)
        yield "r2a"
        next(steps)
        yield "r2x"
        next(steps)
        yield "r2b"
        next(steps, None)
        scaled = final[0] * gain_f
        unit = k.unit[p]
        own_inner = jnp.sum(scaled * unit, axis=1, keepdims=True)
        k.inners[p, g] = jnp.broadcast_to(own_inner, (R, OWN))
        sent = share_g(k.inners.at[p], k.sq_s.at[PARTS + p], k.sq_r.at[PARTS + p])
        yield "in"
        finish(sent)
        inner = jnp.sum(k.inners[p], axis=0)[:, :1] / D
        mg[x, z] = ((scaled - unit * inner) / mixed_rms).astype(BF16)
        steps = gather_tensor(mg, *agt(1), done)
        next(steps)
        yield "mg1"
        next(steps)
        yield "mg2"
        next(steps)
        yield "mgx"
        next(steps, None)
        nhg = k.nhg.at[p]
        nhg[...] = lax.dot_general(
            mg[...].reshape(TOK, WIDE),
            k.proj_h[...],
            (((1,), (1,)), ((), ())),
            preferred_element_type=F32,
        ).reshape(NG, GR, FEAT)
        sent = scatter_g(nhg, k.nhg_recv.at[p], k.ng_s.at[p], k.ng_r.at[p])
        k.nhg_recv[p, g] = nhg[g]
        yield "ng"
        arrive(sent)
        done.extend(sent)
        scaled = jnp.sum(k.nhg_recv[p], axis=0) * gain_h
        unit_rows = own_rows(k.sums[:, :FEAT], p)
        inner = jnp.sum(scaled * unit_rows, axis=1, keepdims=True)
        sent = share_tensor(
            to_tile([inner]), k.last_stats.at[p], k.ls_s.at[p], k.ls_r.at[p]
        )
        yield "ls"
        finish(sent)
        inner = to_col(jnp.sum(k.last_stats[p], axis=0)[:1, :], GR) / D
        hidden_grad = (scaled - unit_rows * inner) / own_rows(k.sums[:, FEAT : FEAT + 1], p)
        k.nhg_recv[p, 0] = hidden_grad

    def head_side():
        def tile(n, carry):
            columns = pl.ds(pl.multiple_of(n * 256, 256), 256)
            total = jnp.zeros((WIDE, 256), F32)
            for p in range(PARTS):
                total = total + jnp.dot(
                    k.flipped[p],
                    k.lg[p, :, :, :, columns].reshape(TOK, 256),
                    preferred_element_type=F32,
                )
            k.head_grad[:, columns] = total.astype(BF16)
            return carry

        lax.fori_loop(0, VOC // 512, tile, 0)
        yield "half"
        lax.fori_loop(VOC // 512, VOC // 256, tile, 0)
        yield

    def proj_side():
        def product(ref, p):
            return lax.dot_general(
                ref[:, :, p * R : (p + 1) * R, :].reshape(TOK, FEAT),
                k.mg[p].reshape(TOK, WIDE),
                (((0,), (0,)), ((), ())),
                preferred_element_type=F32,
            )

        rows = FEAT // NY
        for i, ref in enumerate((k.nh, k.ne)):
            k.core_recv[0, :, :rows, i * WIDE : (i + 1) * WIDE] = product(ref, 0).reshape(
                NY, rows, WIDE
            )
        yield "half"
        for i, (ref, out) in enumerate(((k.nh, k.ph_grad), (k.ne, k.pe_grad))):
            first = k.core_recv[0, :, :rows, i * WIDE : (i + 1) * WIDE].reshape(FEAT, WIDE)
            out[...] = (first + product(ref, 1)).astype(BF16)
        yield

    flows = {"a": chain(0), "b": chain(1), "h": head_side(), "p": proj_side()}
    for step in SCHEDULE:
        name, label = step.split(".")
        for reached in flows[name]:
            if reached == label:
                break
    for one in done:
        one.wait_send()
    for p in range(PARTS):
        for i, (_, dev) in enumerate(g_peers()):
            rcopy(
                k.losses.at[p, g], k.losses.at[p, g], k.lo_s.at[p, i], k.lo_r.at[p, i], dev
            ).wait_recv()
    loss = k.losses[0]
    for p in range(1, PARTS):
        loss = loss + k.losses[p]
    k.loss[...] = jnp.sum(loss, axis=0)[:1, :1] / mask_total
    whole = jnp.concatenate(
        [k.nhg_recv[p, 0].reshape(4, R, FEAT) for p in range(PARTS)], axis=1
    ).reshape(OWN, FEAT)
    k.hidden_grad[...] = whole.T.astype(BF16)


SCHEDULE = (
    "a.rs1a",
    "a.rs1x",
    "b.rs1a",
    "a.rs1b",
    "b.rs1x",
    "a.sq",
    "b.rs1b",
    "a.ag1",
    "a.ag2",
    "b.sq",
    "a.agx",
    "b.ag1",
    "a.ry",
    "b.ag2",
    "b.agx",
    "a.ryx",
    "b.ry",
    "a.st",
    "b.ryx",
    "a.lg",
    "a.lgf",
    "b.st",
    "a.lgc",
    "b.lg",
    "a.r2a",
    "b.lgf",
    "a.r2x",
    "b.lgc",
    "a.r2b",
    "b.r2a",
    "h.half",
    "a.in",
    "b.r2x",
    "a.mg1",
    "h.end",
    "a.mg2",
    "b.r2b",
    "a.mgx",
    "b.in",
    "b.mg1",
    "a.ng",
    "p.half",
    "b.mg2",
    "b.mgx",
    "a.ls",
    "b.ng",
    "p.end",
    "b.ls",
    "a.end",
    "b.end",
)


def vmem(n):
    return [pl.BlockSpec(memory_space=pltpu.VMEM)] * n


def dma(*shape):
    return pltpu.SemaphoreType.DMA(shape)


def pairs(*shapes):
    return [dma(*shape) for shape in shapes for _ in range(2)]


def call(*args):
    return pl.pallas_call(
        kernel,
        out_shape=(
            jax.ShapeDtypeStruct((1, 1), F32),
            jax.ShapeDtypeStruct((FEAT, OWN), BF16),
            jax.ShapeDtypeStruct((FEAT, WIDE), BF16),
            jax.ShapeDtypeStruct((FEAT, WIDE), BF16),
            jax.ShapeDtypeStruct((WIDE, VOC), BF16),
        ),
        in_specs=vmem(7) + [pl.BlockSpec(memory_space=pl.ANY)] * 4,
        out_specs=tuple(vmem(5)),
        scratch_shapes=[
            pltpu.VMEM((FEAT, TABLE), BF16),
            pltpu.VMEM((FEAT, WIDE), BF16),
            pltpu.VMEM((FEAT, WIDE), BF16),
            pltpu.VMEM((WIDE, VOC), BF16),
            dma(4),
            pltpu.VMEM((NG, 8, OWN), F32),
            pltpu.VMEM((NG, 1, OWN), jnp.int32),
            pltpu.VMEM((NG * OWN, 1), jnp.int32),
            pltpu.VMEM((NG, OWN, FEAT), BF16),
            pltpu.VMEM((NG, OWN, FEAT), BF16),
            pltpu.VMEM((NX, NZ, ROWS, FEAT), BF16),
            pltpu.VMEM((NX, NZ, ROWS, FEAT), BF16),
            pltpu.VMEM((PARTS, R, WIDE), F32),
            pltpu.VMEM((PARTS, NX, NZ, R, WIDE), BF16),
            pltpu.VMEM((PARTS, NC, NY, GR, VOC), F32),
            pltpu.VMEM((PARTS, NY, GR, VOC), F32),
            pltpu.VMEM((PARTS, NY - 1, GR, VOC), F32),
            pltpu.VMEM((PARTS, NX, NZ, R, VOC), BF16),
            pltpu.VMEM((PARTS, WIDE, TOK), BF16),
            pltpu.VMEM((PARTS, NX, NZ, R, WIDE), BF16),
            pltpu.VMEM((PARTS, NG, GR, FEAT), F32),
            pltpu.VMEM((PARTS, NG, GR, FEAT), F32),
            pltpu.VMEM((OWN, 256), F32),
        ]
        + reduce_scratch()
        + [
            pltpu.VMEM((NT, 8, OWN), F32),
            pltpu.VMEM((NT, 8, OWN), F32),
            pltpu.VMEM((PARTS, NT, 8, OWN), F32),
            pltpu.VMEM((PARTS, NT, 8, OWN), F32),
            pltpu.VMEM((NG, 8, OWN), F32),
            pltpu.VMEM((PARTS, NG, 8, OWN), F32),
            pltpu.VMEM((PARTS, NG, R, OWN), F32),
            pltpu.VMEM((PARTS, NG, R, OWN), F32),
        ]
        + pairs((NG - 1,), (NG - 1,))
        + [pltpu.SemaphoreType.DMA] * 4
        + pairs((NG - 1,), (2, 4), (2, 4), (NG - 1,))
        + pairs((PARTS, 2, NZ), (PARTS, 2, NZ), (2 * PARTS, NG - 1))
        + pairs((PARTS, 2, NZ), (PARTS, 2, NZ))
        + pairs((PARTS, CHUNKS), (PARTS, 6), (PARTS,), (PARTS, NG - 1))
        + pairs((PARTS, 4), (PARTS, 4), (PARTS, NG - 1), (PARTS,)),
        compiler_params=pltpu.CompilerParams(
            collective_id=0, has_side_effects=True, vmem_limit_bytes=VMEM_LIMIT
        ),
        name="whole",
    )(*args)


def settle_kernel(a, b, c, d, a_out, b_out, c_out, d_out):
    @pl.when(pl.program_id(0) == 0)
    def _():
        a_out[...] = a[...]
        b_out[...] = b[...]
        c_out[...] = c[...]

    d_out[...] = d[...]


def settle(*arrays):
    blocks = 4
    specs = [pl.BlockSpec(a.shape, lambda i: (0, 0)) for a in arrays[:3]]
    specs.append(pl.BlockSpec((WIDE // blocks, VOC), lambda i: (i, 0)))
    return pl.pallas_call(
        settle_kernel,
        grid=(blocks,),
        out_shape=tuple(jax.ShapeDtypeStruct(a.shape, a.dtype) for a in arrays),
        in_specs=specs,
        out_specs=tuple(specs),
        compiler_params=pltpu.CompilerParams(vmem_limit_bytes=VMEM_LIMIT),
        name="settle",
    )(*arrays)


def per_device(
    hidden_prev,
    next_ids,
    targets,
    loss_mask,
    gain_hidden,
    gain_embed,
    gain_final,
    embed_table,
    proj_hidden,
    proj_embed,
    head_weight,
):
    loss, hidden_grad, ph_grad, pe_grad, head_grad = call(
        hidden_prev.T,
        next_ids[None, :],
        targets[None, :],
        loss_mask[None, :],
        gain_hidden,
        gain_embed,
        gain_final,
        embed_table.T,
        proj_hidden,
        proj_embed,
        head_weight,
    )
    hidden_grad, ph_grad, pe_grad, head_grad = settle(hidden_grad, ph_grad, pe_grad, head_grad)
    return (loss[0, 0], hidden_grad.T, ph_grad, pe_grad, head_grad)


def solution(mesh):
    return jax.shard_map(
        per_device,
        mesh=mesh,
        in_specs=(
            P(("context", "dp"), "tensor"),
            P(("context", "dp")),
            P(("context", "dp")),
            P(("context", "dp")),
            P("tensor"),
            P("tensor"),
            P(("context", "dp")),
            P(("context", "dp"), "tensor"),
            P("tensor", ("context", "dp")),
            P("tensor", ("context", "dp")),
            P(("context", "dp"), "tensor"),
        ),
        out_specs=(
            P(),
            P(("context", "dp"), "tensor"),
            P("tensor", ("context", "dp")),
            P("tensor", ("context", "dp")),
            P(("context", "dp"), "tensor"),
        ),
        check_vma=False,
    )
```
